512 devices in a mesh: ctx: 32 (over z, x_lo), ch: 16 (over y, x_hi, core).
Axes of the slice: x: 4 (x_hi: 2, x_lo: 2; x = x_hi * 2 + x_lo), y: 4, z: 16, core: 2. Of those that a mesh axis runs over, the one named last changes fastest.
Arguments:
- query: bfloat16 [4096, 4096], P('ch', 'ctx'), may hold values from -6 to 6
- key_gate: bfloat16 [4096, 4096], P('ch', 'ctx'), may hold values from -6 to 6
- value_in: bfloat16 [4096, 4096], P('ch', 'ctx'), may hold values from -6 to 6
- grad_output: bfloat16 [4096, 4096], P('ch', 'ctx'), may hold values from -6 to 6
- residue: float32 [4096, 16], P('ch'), may hold values from -4 to 4
- log_rate: float32 [4096, 16], P('ch'), may hold values from -1.386 to 6.685
Outputs:
- grad_query: bfloat16 [4096, 4096], P('ch', 'ctx')
- grad_key: bfloat16 [4096, 4096], P('ch', 'ctx')
- grad_value: bfloat16 [4096, 4096], P('ch', 'ctx')
- grad_residue: float32 [4096, 16], P('ch')
- grad_log_rate: float32 [4096, 16], P('ch')
The draws below stay inside these ranges and needn't reach their ends.
All inputs are finite; a program needn't handle non-finite values.
Results may differ from the reference program's by a relative error of at most 0.0122.
Values may be sent and summed in bfloat16 or wider, within the bound.
No kernel may reach another device: no remote copies, remote signals or barrier semaphores. Data moves between devices by JAX's collectives and lax.ppermute only.
A program may use at most 64 MiB of HBM per device.

```python
import math
import jax
import jax.numpy as jnp
from jax import lax

POLES = 16
TOKENS = 4096
CHANNELS = 4096


def level_of(key, shape, split, smallest, high):
    loudness = 1.0
    for axis_at, parts in split:
        steps = jax.random.uniform(jax.random.fold_in(jax.random.fold_in(key, 6), axis_at), (parts,), jnp.float32, smallest / len(split), high / len(split))
        loudness = loudness * jnp.repeat(jnp.exp(steps), shape[axis_at] // parts).reshape((-1,) + (1,) * (len(shape) - 1 - axis_at))
    return loudness


def bell_draw(own_key, dims, deviation, bound, shards=(), held_as=jnp.bfloat16):
    array = deviation * jax.random.normal(own_key, dims, jnp.float32)
    if shards:
        array = array * level_of(own_key, dims, shards, -0.22, 0.18)
    return jnp.clip(array, -bound, bound).astype(held_as)


def setup_inputs(seed: int = 0) -> dict:
    seeds = jax.random.split(jax.random.key(seed), 7)
    return {
        "query": bell_draw(seeds[0], (CHANNELS, TOKENS), 1.0, 6.0, ((0, 16), (1, 32))),
        "key_gate": bell_draw(seeds[1], (CHANNELS, TOKENS), 1.0, 6.0, ((0, 16), (1, 32))),
        "value_in": bell_draw(seeds[2], (CHANNELS, TOKENS), 1.0, 6.0, ((0, 16), (1, 32))),
        "grad_output": bell_draw(seeds[3], (CHANNELS, TOKENS), 1.0, 6.0, ((0, 16), (1, 32))),
        "residue": bell_draw(seeds[4], (CHANNELS, POLES), 1.0, 4.0, ((0, 16),), jnp.float32),
        "log_rate": jnp.clip(-1.386 + 8.071 * jax.random.uniform(seeds[5], (CHANNELS, POLES), jnp.float32) ** level_of(seeds[5], (CHANNELS, POLES), ((0, 16),), -0.2, 0.2), -1.386, 6.685),
    }


def reference(query, key_gate, value_in, grad_output, residue, log_rate):
    mixed_input = (key_gate.astype(jnp.float32) * value_in.astype(jnp.float32)).astype(jnp.bfloat16)
    grad_conv = (query.astype(jnp.float32) * grad_output.astype(jnp.float32)).astype(jnp.bfloat16)
    total_len = 2 * TOKENS
    norm_factor = 1.0 / math.sqrt(TOKENS)

    def per_channel(items):
        mixed_row, grad_row, residue_row, log_row = items
        times = jnp.arange(TOKENS, dtype=jnp.float32)
        rates = jnp.exp(log_row) / TOKENS
        exponent = rates[:, None] * times[None, :]
        decay_table = jnp.exp(-exponent)
        filt = lax.optimization_barrier(jnp.sum(residue_row[:, None] * decay_table, axis=0)) * norm_factor
        mixed_spec = jnp.fft.rfft(mixed_row.astype(jnp.float32), n=total_len)
        grad_spec = jnp.fft.rfft(grad_row.astype(jnp.float32), n=total_len)
        filt_spec = jnp.fft.rfft(filt, n=total_len)
        conv_row = jnp.fft.irfft(mixed_spec * filt_spec, n=total_len)[:TOKENS]
        input_grad = jnp.fft.irfft(grad_spec * jnp.conj(filt_spec), n=total_len)[:TOKENS]
        filt_grad = jnp.fft.irfft(grad_spec * jnp.conj(mixed_spec), n=total_len)[:TOKENS]
        grad_res = lax.optimization_barrier(jnp.sum(filt_grad[None, :] * decay_table, axis=1)) / TOKENS
        grad_log = -(residue_row / TOKENS) * lax.optimization_barrier(jnp.sum(filt_grad[None, :] * decay_table * exponent, axis=1))
        return (conv_row, input_grad, grad_res, grad_log)
    conv_out, grad_mixed, grad_residue, grad_log_rate = lax.map(per_channel, (mixed_input, grad_conv, residue, log_rate))
    conv_out = conv_out.astype(jnp.bfloat16)
    grad_mixed = grad_mixed.astype(jnp.bfloat16)
    grad_query = (grad_output.astype(jnp.float32) * conv_out.astype(jnp.float32)).astype(jnp.bfloat16)
    grad_key = (grad_mixed.astype(jnp.float32) * value_in.astype(jnp.float32)).astype(jnp.bfloat16)
    grad_value = (grad_mixed.astype(jnp.float32) * key_gate.astype(jnp.float32)).astype(jnp.bfloat16)
    return (grad_query, grad_key, grad_value, grad_residue.astype(jnp.float32), grad_log_rate.astype(jnp.float32))
```

```python
import functools

import jax
import jax.numpy as jnp
from jax import lax
from jax.experimental import pallas as pl
from jax.experimental.pallas import tpu as pltpu
from jax.sharding import PartitionSpec as P

F32 = jnp.float32
BF16 = jnp.bfloat16
POLES = 16
BLOCK = 8
LANES = 128


def gated(left_ref, right_ref):
    product = (left_ref[...].astype(F32) * right_ref[...].astype(F32)).astype(BF16)
    return product.astype(F32).T


def pole_rows(residue_ref, log_ref):
    channels = residue_ref.shape[0]
    filler = jnp.zeros((channels, LANES - 2 * POLES), F32)
    both = jnp.concatenate([residue_ref[...], log_ref[...], filler], axis=1).T
    return both[:POLES], both[POLES : 2 * POLES]


def summary_kernel(length, key_ref, value_ref, query_ref, out_grad_ref, residue_ref, log_ref, out_ref, mixed, grad):
    width, channels = mixed.shape
    mixed[...] = gated(key_ref, value_ref)
    grad[...] = gated(query_ref, out_grad_ref)
    _, log_rows = pole_rows(residue_ref, log_ref)
    decay = jnp.exp(-(jnp.exp(log_rows) / length))
    zero = jnp.zeros((POLES, channels), F32)

    def step(block, carry):
        state, moment, res, rate, back, back_moment = carry
        first = block * BLOCK
        for row in range(BLOCK):
            mixed_row = mixed[pl.ds(first + row, 1), :]
            grad_row = grad[pl.ds(first + row, 1), :]
            late_row = grad[pl.ds(width - 1 - first - row, 1), :]
            faded = decay * state
            state = faded + mixed_row
            moment = decay * moment + faded
            res = res + grad_row * state
            rate = rate + grad_row * moment
            faded = decay * back
            back = faded + late_row
            back_moment = decay * back_moment + faded
        return state, moment, res, rate, back, back_moment

    state, moment, res, rate, back, back_moment = lax.fori_loop(0, width // BLOCK, step, (zero,) * 6)
    last = decay * state
    last_moment = decay * moment + last
    rows = [last, back, last_moment, back_moment, res, rate, zero, zero]
    out_ref[...] = jnp.concatenate(rows, axis=0).T.reshape(out_ref.shape)


def local_kernel(
    length,
    place_ref,
    key_ref,
    value_ref,
    query_ref,
    out_grad_ref,
    residue_ref,
    log_ref,
    conv_ref,
    back_ref,
    ahead_ref,
    behind_ref,
    fade_ref,
    chunk_ref,
    mixed,
    grad,
):
    width, channels = mixed.shape
    mixed[...] = gated(key_ref, value_ref)
    grad[...] = gated(query_ref, out_grad_ref)
    residue_rows, log_rows = pole_rows(residue_ref, log_ref)
    rates = jnp.exp(log_rows) / length
    decay = jnp.exp(-rates)
    weight = residue_rows * (length**-0.5)
    zero = jnp.zeros((POLES, channels), F32)

    def step(block, carry):
        state, back = carry
        first = pl.multiple_of(block * BLOCK, BLOCK)
        last = pl.multiple_of(width - BLOCK - block * BLOCK, BLOCK)
        ahead, behind = [], []
        for row in range(BLOCK):
            state = decay * state + mixed[pl.ds(first + row, 1), :]
            ahead.append(jnp.sum(weight * state, axis=0, keepdims=True))
            back = decay * back + grad[pl.ds(last + BLOCK - 1 - row, 1), :]
            behind.append(jnp.sum(weight * back, axis=0, keepdims=True))
        conv_ref[pl.ds(first, BLOCK), :] = jnp.concatenate(ahead, axis=0)
        back_ref[pl.ds(last, BLOCK), :] = jnp.concatenate(behind[::-1], axis=0)
        return state, back

    lax.fori_loop(0, width // BLOCK, step, (zero, zero))
    steps = lax.broadcasted_iota(jnp.int32, (BLOCK, channels), 0).astype(F32)
    for pole in range(POLES):
        rate = rates[pole : pole + 1]
        scale = weight[pole : pole + 1]
        ahead_ref[pole] = scale * jnp.exp(-(rate * steps))
        behind_ref[pole] = scale * jnp.exp(-(rate * (BLOCK - steps)))
    fade_ref[...] = jnp.exp(-(rates * BLOCK))
    own = log_ref[pl.ds(pl.multiple_of(place_ref[0] * BLOCK, BLOCK), BLOCK), :]
    own_rates = jnp.exp(jnp.concatenate([own] * (LANES // POLES), axis=1)) / length
    chunk_ref[...] = jnp.exp(-(own_rates * width))


def prefix_kernel(width, parts_ref, chunk_ref, out_ref):
    chunks = parts_ref.shape[0]
    fade = chunk_ref[...]
    lane = lax.broadcasted_iota(jnp.int32, fade.shape, 1)
    zero = jnp.zeros(fade.shape, F32)

    def shifted(part, places):
        return pltpu.roll(part, LANES - places * POLES, 1)

    parts = [parts_ref[chunk] for chunk in range(chunks)]
    state, moment, res, rate = zero, zero, zero, zero
    states = []
    for part in parts:
        states.append(state)
        back = shifted(part, 1)
        res = res + back * state
        rate = rate + shifted(part, 3) * state + back * moment
        moment = fade * (moment + width * state) + shifted(part, 2)
        state = fade * state + part
    local = functools.reduce(lambda a, b: a + b, parts)
    totals = pltpu.roll(res, 2 * POLES, 1)
    totals = jnp.where(lane < 3 * POLES, totals, pltpu.roll(rate, 3 * POLES, 1))
    totals = totals + pltpu.roll(local, LANES - 2 * POLES, 1)
    back = zero
    for chunk in range(chunks - 1, -1, -1):
        sent = jnp.where(lane < POLES, states[chunk], jnp.where(lane < 2 * POLES, back, totals))
        out_ref[chunk] = sent
        back = fade * back + parts[chunk]


def output_kernel(
    length,
    carried_ref,
    conv_ref,
    back_ref,
    ahead_ref,
    behind_ref,
    fade_ref,
    key_ref,
    value_ref,
    out_grad_ref,
    residue_ref,
    log_ref,
    query_out,
    key_out,
    value_out,
    residue_out,
    log_out,
):
    channels = residue_ref.shape[0]
    width = conv_ref.shape[0]
    blocks = width // BLOCK
    carried = carried_ref[...].reshape(channels, LANES)
    rows = carried.T
    residue_out[...] = carried[:, 2 * POLES : 3 * POLES] * (1.0 / length)
    rates = jnp.exp(log_ref[...]) / length
    log_out[...] = -(residue_ref[...] / length) * rates * carried[:, 3 * POLES : 4 * POLES]
    for half in range(channels // LANES):
        here = slice(half * LANES, (half + 1) * LANES)
        total = [conv_ref[block * BLOCK : (block + 1) * BLOCK, here] for block in range(blocks)]
        for pole in range(POLES):
            term = ahead_ref[pole, :, here] * rows[pole : pole + 1, here]
            fade = fade_ref[pole : pole + 1, here]
            for block in range(blocks):
                total[block] = total[block] + term
                term = term * fade
        conv = jnp.concatenate(total, axis=0).T.astype(BF16).astype(F32)
        query_out[here, :] = (out_grad_ref[here, :].astype(F32) * conv).astype(BF16)
        total = [back_ref[block * BLOCK : (block + 1) * BLOCK, here] for block in range(blocks)]
        for pole in range(POLES):
            term = behind_ref[pole, :, here] * rows[POLES + pole : POLES + pole + 1, here]
            fade = fade_ref[pole : pole + 1, here]
            for block in range(blocks - 1, -1, -1):
                total[block] = total[block] + term
                term = term * fade
        back = jnp.concatenate(total, axis=0).T.astype(BF16).astype(F32)
        key_out[here, :] = (back * value_ref[here, :].astype(F32)).astype(BF16)
        value_out[here, :] = (back * key_ref[here, :].astype(F32)).astype(BF16)


def on_device(query, key_gate, value_in, grad_output, residue, log_rate):
    chunks = lax.axis_size("ctx")
    channels, width = query.shape
    length = width * chunks
    struct = jax.ShapeDtypeStruct
    in_vmem = pl.BlockSpec(memory_space=pltpu.VMEM)
    turned = [pltpu.VMEM((width, channels), F32)] * 2
    params = pltpu.CompilerParams(vmem_limit_bytes=32 * 1024 * 1024)
    gates = (key_gate, value_in, query, grad_output, residue, log_rate)
    sent = struct((chunks, channels // chunks, LANES), F32)

    summary = pl.pallas_call(
        functools.partial(summary_kernel, float(length)),
        out_shape=sent,
        in_specs=[in_vmem] * 6,
        out_specs=in_vmem,
        scratch_shapes=turned,
        compiler_params=params,
        name="chunk_summary",
    )(*gates)
    parts = lax.all_to_all(summary, "ctx", split_axis=0, concat_axis=0, tiled=True)
    place = lax.axis_index("ctx").astype(jnp.int32).reshape(1)
    conv, back, ahead, behind, fade, chunk_fade = pl.pallas_call(
        functools.partial(local_kernel, float(length)),
        out_shape=(
            struct((width, channels), F32),
            struct((width, channels), F32),
            struct((POLES, BLOCK, channels), F32),
            struct((POLES, BLOCK, channels), F32),
            struct((POLES, channels), F32),
            struct((BLOCK, LANES), F32),
        ),
        in_specs=[pl.BlockSpec(memory_space=pltpu.SMEM)] + [in_vmem] * 6,
        out_specs=[in_vmem] * 6,
        scratch_shapes=turned,
        compiler_params=params,
        name="local_part",
        cost_estimate=pl.CostEstimate(flops=20_000_000, bytes_accessed=1_500_000, transcendentals=0),
    )(place, *gates)
    carried = pl.pallas_call(
        functools.partial(prefix_kernel, float(width)),
        out_shape=sent,
        in_specs=[in_vmem] * 2,
        out_specs=in_vmem,
        compiler_params=params,
        name="chunk_prefix",
    )(parts, chunk_fade)
    carried = lax.all_to_all(carried, "ctx", split_axis=0, concat_axis=0, tiled=True)
    gate_out = struct((channels, width), BF16)
    pole_out = struct((channels, POLES), F32)
    return pl.pallas_call(
        functools.partial(output_kernel, float(length)),
        out_shape=(gate_out, gate_out, gate_out, pole_out, pole_out),
        in_specs=[in_vmem] * 11,
        out_specs=[in_vmem] * 5,
        compiler_params=params,
        name="outputs",
    )(carried, conv, back, ahead, behind, fade, key_gate, value_in, grad_output, residue, log_rate)


def solution(mesh):
    both = P("ch", "ctx")
    rows = P("ch", None)
    return jax.shard_map(
        on_device,
        mesh=mesh,
        in_specs=(both, both, both, both, rows, rows),
        out_specs=(both, both, both, rows, rows),
        check_vma=False,
    )
```

```python
import functools

import jax
import jax.numpy as jnp
from jax import lax
from jax.experimental import pallas as pl
from jax.experimental.pallas import tpu as pltpu
from jax.sharding import PartitionSpec as P

F32 = jnp.float32
BF16 = jnp.bfloat16
POLES = 16
BLOCK = 8
LANES = 128


def gated(left_ref, right_ref):
    product = (left_ref[...].astype(F32) * right_ref[...].astype(F32)).astype(BF16)
    return product.astype(F32).T


def rounded(value):
    return value.astype(BF16).astype(F32)


def summary_kernel(length, key_ref, value_ref, query_ref, out_grad_ref, log_ref, out_ref, mixed, grad):
    width, channels = mixed.shape
    mixed[...] = gated(key_ref, value_ref)
    grad[...] = gated(query_ref, out_grad_ref)
    decay = jnp.exp(-(jnp.exp(log_ref[...]) / length))
    zero = jnp.zeros((POLES, channels), F32)

    def step(block, carry):
        state, moment, res, rate, back, back_moment = carry
        first = block * BLOCK
        for row in range(BLOCK):
            mixed_row = mixed[pl.ds(first + row, 1), :]
            grad_row = grad[pl.ds(first + row, 1), :]
            late_row = grad[pl.ds(width - 1 - first - row, 1), :]
            faded = decay * state
            state = faded + mixed_row
            moment = decay * moment + faded
            res = res + grad_row * state
            rate = rate + grad_row * moment
            faded = decay * back
            back = faded + late_row
            back_moment = decay * back_moment + faded
        return state, moment, res, rate, back, back_moment

    state, moment, res, rate, back, back_moment = lax.fori_loop(0, width // BLOCK, step, (zero,) * 6)
    last = decay * state
    last_moment = decay * moment + last
    rest = [last - rounded(last), back - rounded(back)]
    rows = [last, back, last_moment, back_moment, res, rate] + rest
    out_ref[...] = jnp.concatenate(rows, axis=0).T.astype(BF16)


def local_kernel(
    length,
    place_ref,
    key_ref,
    value_ref,
    query_ref,
    out_grad_ref,
    residue_ref,
    log_ref,
    conv_ref,
    back_ref,
    ahead_ref,
    behind_ref,
    fade_ref,
    chunk_ref,
    mixed,
    grad,
    logs,
):
    width, channels = mixed.shape
    mixed[...] = gated(key_ref, value_ref)
    grad[...] = gated(query_ref, out_grad_ref)
    rates = jnp.exp(log_ref[...]) / length
    decay = jnp.exp(-rates)
    weight = residue_ref[...] * (length**-0.5)
    zero = jnp.zeros((POLES, channels), F32)

    def step(block, carry):
        state, back = carry
        first = pl.multiple_of(block * BLOCK, BLOCK)
        last = pl.multiple_of(width - BLOCK - block * BLOCK, BLOCK)
        ahead, behind = [], []
        for row in range(BLOCK):
            state = decay * state + mixed[pl.ds(first + row, 1), :]
            ahead.append(jnp.sum(weight * state, axis=0, keepdims=True))
            back = decay * back + grad[pl.ds(last + BLOCK - 1 - row, 1), :]
            behind.append(jnp.sum(weight * back, axis=0, keepdims=True))
        conv_ref[pl.ds(first, BLOCK), :] = jnp.concatenate(ahead, axis=0)
        back_ref[pl.ds(last, BLOCK), :] = jnp.concatenate(behind[::-1], axis=0)
        return state, back

    lax.fori_loop(0, width // BLOCK, step, (zero, zero))
    steps = lax.broadcasted_iota(jnp.int32, (BLOCK, channels), 0).astype(F32)
    for pole in range(POLES):
        rate = rates[pole : pole + 1]
        scale = weight[pole : pole + 1]
        ahead_ref[pole] = scale * jnp.exp(-(rate * steps))
        behind_ref[pole] = scale * jnp.exp(-(rate * (BLOCK - steps)))
    fade_ref[...] = jnp.exp(-(rates * BLOCK))
    logs[...] = jnp.concatenate([log_ref[...]] * (LANES // POLES), axis=0).T
    own = logs[pl.ds(pl.multiple_of(place_ref[0] * BLOCK, BLOCK), BLOCK), :]
    chunk_ref[...] = jnp.exp(-(jnp.exp(own) / length * width))


def prefix_kernel(width, parts_ref, chunk_ref, out_ref):
    chunks = parts_ref.shape[0] // BLOCK
    fade = chunk_ref[...]
    lane = lax.broadcasted_iota(jnp.int32, fade.shape, 1)
    zero = jnp.zeros(fade.shape, F32)

    def shifted(part, places):
        return pltpu.roll(part, LANES - places * POLES, 1)

    parts = []
    for pair in range(chunks // 2):
        both = parts_ref[pair * 2 * BLOCK : (pair + 1) * 2 * BLOCK, :].astype(F32)
        parts += [both[:BLOCK], both[BLOCK:]]
    ends = [part + shifted(part, 6) for part in parts]
    state, moment, res, rate = zero, zero, zero, zero
    states = []
    for part, end in zip(parts, ends):
        states.append(state)
        back = shifted(end, 1)
        res = res + back * state
        rate = rate + shifted(part, 3) * state + back * moment
        moment = fade * (moment + width * state) + shifted(part, 2)
        state = fade * state + end
    local = functools.reduce(lambda a, b: a + b, parts)
    totals = jnp.where(lane < 3 * POLES, pltpu.roll(res, 2 * POLES, 1), pltpu.roll(rate, 3 * POLES, 1))
    totals = totals + shifted(local, 2)
    back = zero
    sent = [None] * chunks
    for chunk in range(chunks - 1, -1, -1):
        whole = jnp.where(lane < POLES, states[chunk], jnp.where(lane < 2 * POLES, back, totals))
        rest = pltpu.roll(whole - rounded(whole), LANES // 2, 1)
        sent[chunk] = jnp.where(lane < LANES // 2, whole, rest)
        back = fade * back + ends[chunk]
    for pair in range(chunks // 2):
        both = jnp.concatenate(sent[2 * pair : 2 * pair + 2], axis=0)
        out_ref[pair * 2 * BLOCK : (pair + 1) * 2 * BLOCK, :] = both.astype(BF16)


def output_kernel(
    length,
    carried_ref,
    conv_ref,
    back_ref,
    ahead_ref,
    behind_ref,
    fade_ref,
    key_ref,
    value_ref,
    out_grad_ref,
    residue_ref,
    log_ref,
    query_out,
    key_out,
    value_out,
    residue_out,
    log_out,
):
    width, channels = conv_ref.shape
    blocks = width // BLOCK
    rows = carried_ref[...].astype(F32).T
    rows = rows[: LANES // 2] + rows[LANES // 2 :]
    residue_out[...] = rows[2 * POLES : 3 * POLES] * (1.0 / length)
    rates = jnp.exp(log_ref[...]) / length
    log_out[...] = -(residue_ref[...] / length) * rates * rows[3 * POLES :]
    for half in range(channels // LANES):
        here = slice(half * LANES, (half + 1) * LANES)
        total = [conv_ref[block * BLOCK : (block + 1) * BLOCK, here] for block in range(blocks)]
        for pole in range(POLES):
            term = ahead_ref[pole, :, here] * rows[pole : pole + 1, here]
            fade = fade_ref[pole : pole + 1, here]
            for block in range(blocks):
                total[block] = total[block] + term
                term = term * fade
        conv = jnp.concatenate(total, axis=0).T.astype(BF16).astype(F32)
        query_out[here, :] = (out_grad_ref[here, :].astype(F32) * conv).astype(BF16)
        total = [back_ref[block * BLOCK : (block + 1) * BLOCK, here] for block in range(blocks)]
        for pole in range(POLES):
            term = behind_ref[pole, :, here] * rows[POLES + pole : POLES + pole + 1, here]
            fade = fade_ref[pole : pole + 1, here]
            for block in range(blocks - 1, -1, -1):
                total[block] = total[block] + term
                term = term * fade
        back = jnp.concatenate(total, axis=0).T.astype(BF16).astype(F32)
        key_out[here, :] = (back * value_ref[here, :].astype(F32)).astype(BF16)
        value_out[here, :] = (back * key_ref[here, :].astype(F32)).astype(BF16)


def on_device(query, key_gate, value_in, grad_output, residue, log_rate):
    chunks = lax.axis_size("ctx")
    channels, width = query.shape
    length = width * chunks
    struct = jax.ShapeDtypeStruct
    in_vmem = pl.BlockSpec(memory_space=pltpu.VMEM)
    turned = [pltpu.VMEM((width, channels), F32)] * 2
    params = pltpu.CompilerParams(vmem_limit_bytes=32 * 1024 * 1024)
    gates = (key_gate, value_in, query, grad_output)
    poles = (residue.T, log_rate.T)
    sent = struct((channels, LANES), BF16)
    per_chunk = (chunks, channels // chunks, LANES)

    def exchange(table):
        table = lax.all_to_all(table.reshape(per_chunk), "ctx", split_axis=0, concat_axis=0, tiled=True)
        return table.reshape(channels, LANES)

    summary = pl.pallas_call(
        functools.partial(summary_kernel, float(length)),
        out_shape=sent,
        in_specs=[in_vmem] * 5,
        out_specs=in_vmem,
        scratch_shapes=turned,
        compiler_params=params,
        name="chunk_summary",
    )(*gates, poles[1])
    parts = exchange(summary)
    place = lax.axis_index("ctx").astype(jnp.int32).reshape(1)
    conv, back, ahead, behind, fade, chunk_fade = pl.pallas_call(
        functools.partial(local_kernel, float(length)),
        out_shape=(
            struct((width, channels), F32),
            struct((width, channels), F32),
            struct((POLES, BLOCK, channels), F32),
            struct((POLES, BLOCK, channels), F32),
            struct((POLES, channels), F32),
            struct((BLOCK, LANES), F32),
        ),
        in_specs=[pl.BlockSpec(memory_space=pltpu.SMEM)] + [in_vmem] * 6,
        out_specs=[in_vmem] * 6,
        scratch_shapes=turned + [pltpu.VMEM((channels, LANES), F32)],
        compiler_params=params,
        name="local_part",
        cost_estimate=pl.CostEstimate(flops=20_000_000, bytes_accessed=1_500_000, transcendentals=0),
    )(place, *gates, *poles)
    carried = pl.pallas_call(
        functools.partial(prefix_kernel, float(width)),
        out_shape=sent,
        in_specs=[in_vmem] * 2,
        out_specs=in_vmem,
        compiler_params=params,
        name="chunk_prefix",
    )(parts, chunk_fade)
    carried = exchange(carried)
    gate_out = struct((channels, width), BF16)
    pole_out = struct((POLES, channels), F32)
    outs = pl.pallas_call(
        functools.partial(output_kernel, float(length)),
        out_shape=(gate_out, gate_out, gate_out, pole_out, pole_out),
        in_specs=[in_vmem] * 11,
        out_specs=[in_vmem] * 5,
        compiler_params=params,
        name="outputs",
    )(carried, conv, back, ahead, behind, fade, key_gate, value_in, grad_output, *poles)
    return (*outs[:3], outs[3].T, outs[4].T)


def solution(mesh):
    both = P("ch", "ctx")
    rows = P("ch", None)
    return jax.shard_map(
        on_device,
        mesh=mesh,
        in_specs=(both, both, both, both, rows, rows),
        out_specs=(both, both, both, rows, rows),
        check_vma=False,
    )
```

```python
import functools

import jax
import jax.numpy as jnp
from jax import lax
from jax.experimental import pallas as pl
from jax.experimental.pallas import tpu as pltpu
from jax.sharding import PartitionSpec as P

F32 = jnp.float32
BF16 = jnp.bfloat16
POLES = 16
BLOCK = 8
LANES = 128
MIB = 1024 * 1024


def gated(left_ref, right_ref):
    product = (left_ref[...].astype(F32) * right_ref[...].astype(F32)).astype(BF16)
    return product.astype(F32).T


def rounded(value):
    return value.astype(BF16).astype(F32)


def load_gates(sources, held, sems, mixed, grad):
    copies = [pltpu.make_async_copy(src, dst, sems.at[n]) for n, (src, dst) in enumerate(zip(sources, held))]
    for copy in copies:
        copy.start()
    copies[0].wait()
    copies[1].wait()
    mixed[...] = gated(held[0], held[1])
    copies[2].wait()
    copies[3].wait()
    grad[...] = gated(held[2], held[3])
    for copy in copies[4:]:
        copy.wait()


def summary_kernel(length, *refs):
    sources, (out_ref, mixed, grad, sems), held = refs[:5], refs[5:9], refs[9:]
    load_gates(sources, held, sems, mixed, grad)
    log_ref = held[4]
    width, channels = mixed.shape
    decay = jnp.exp(-(jnp.exp(log_ref[...]) / length))
    zero = jnp.zeros((POLES, channels), F32)

    def step(block, carry):
        state, moment, res, rate, back, back_moment = carry
        first = block * BLOCK
        for row in range(BLOCK):
            mixed_row = mixed[pl.ds(first + row, 1), :]
            grad_row = grad[pl.ds(first + row, 1), :]
            late_row = grad[pl.ds(width - 1 - first - row, 1), :]
            faded = decay * state
            state = faded + mixed_row
            moment = decay * moment + faded
            res = res + grad_row * state
            rate = rate + grad_row * moment
            faded = decay * back
            back = faded + late_row
            back_moment = decay * back_moment + faded
        return state, moment, res, rate, back, back_moment

    state, moment, res, rate, back, back_moment = lax.fori_loop(0, width // BLOCK, step, (zero,) * 6)
    last = decay * state
    last_moment = decay * moment + last
    rest = [last - rounded(last), back - rounded(back)]
    rows = [last, back, last_moment, back_moment, res, rate] + rest
    out_ref[...] = jnp.concatenate(rows, axis=0).T.astype(BF16)


def local_kernel(length, places, index_ref, *refs):
    sources, outs, (mixed, grad, logs, sems), held = refs[:6], refs[6:12], refs[12:16], refs[16:]
    load_gates(sources, held, sems, mixed, grad)
    log_ref, residue_ref = held[4:]
    conv_ref, back_ref, ahead_ref, behind_ref, fade_ref, chunk_ref = outs
    width, channels = mixed.shape
    rates = jnp.exp(log_ref[...]) / length
    decay = jnp.exp(-rates)
    weight = residue_ref[...] * (length**-0.5)
    zero = jnp.zeros((POLES, channels), F32)

    def step(block, carry):
        state, back = carry
        first = pl.multiple_of(block * BLOCK, BLOCK)
        last = pl.multiple_of(width - BLOCK - block * BLOCK, BLOCK)
        ahead, behind = [], []
        for row in range(BLOCK):
            state = decay * state + mixed[pl.ds(first + row, 1), :]
            ahead.append(jnp.sum(weight * state, axis=0, keepdims=True))
            back = decay * back + grad[pl.ds(last + BLOCK - 1 - row, 1), :]
            behind.append(jnp.sum(weight * back, axis=0, keepdims=True))
        conv_ref[pl.ds(first, BLOCK), :] = jnp.concatenate(ahead, axis=0)
        back_ref[pl.ds(last, BLOCK), :] = jnp.concatenate(behind[::-1], axis=0)
        return state, back

    lax.fori_loop(0, width // BLOCK, step, (zero, zero))
    steps = lax.broadcasted_iota(jnp.int32, (BLOCK, channels), 0).astype(F32)
    for pole in range(POLES):
        rate = rates[pole : pole + 1]
        scale = weight[pole : pole + 1]
        ahead_ref[pole] = scale * jnp.exp(-(rate * steps))
        behind_ref[pole] = scale * jnp.exp(-(rate * (BLOCK - steps)))
    fade_ref[...] = jnp.exp(-(rates * BLOCK))
    logs[...] = jnp.concatenate([log_ref[...]] * (LANES // POLES), axis=0).T
    place = 0
    for member, at in enumerate(places):
        place = jnp.where(index_ref[0] == member, at, place)
    own = logs[pl.ds(pl.multiple_of(place * BLOCK, BLOCK), BLOCK), :]
    chunk_ref[...] = jnp.exp(-(jnp.exp(own) / length * width))


def prefix_kernel(width, places, parts_ref, chunk_ref, out_ref):
    chunks = parts_ref.shape[0] // BLOCK
    fade = chunk_ref[...]
    lane = lax.broadcasted_iota(jnp.int32, fade.shape, 1)
    zero = jnp.zeros(fade.shape, F32)

    def shifted(part, places):
        return pltpu.roll(part, LANES - places * POLES, 1)

    parts = []
    for pair in range(chunks // 2):
        both = parts_ref[pair * 2 * BLOCK : (pair + 1) * 2 * BLOCK, :].astype(F32)
        parts += [both[:BLOCK], both[BLOCK:]]
    parts = [parts[at] for at in places]
    ends = [part + shifted(part, 6) for part in parts]
    state, moment, res, rate = zero, zero, zero, zero
    states = []
    for part, end in zip(parts, ends):
        states.append(state)
        back = shifted(end, 1)
        res = res + back * state
        rate = rate + shifted(part, 3) * state + back * moment
        moment = fade * (moment + width * state) + shifted(part, 2)
        state = fade * state + end
    local = functools.reduce(lambda a, b: a + b, parts)
    totals = jnp.where(lane < 3 * POLES, pltpu.roll(res, 2 * POLES, 1), pltpu.roll(rate, 3 * POLES, 1))
    totals = totals + shifted(local, 2)
    back = zero
    sent = [None] * chunks
    for chunk in range(chunks - 1, -1, -1):
        whole = jnp.where(lane < POLES, states[chunk], jnp.where(lane < 2 * POLES, back, totals))
        rest = pltpu.roll(whole - rounded(whole), LANES // 2, 1)
        sent[chunk] = jnp.where(lane < LANES // 2, whole, rest)
        back = fade * back + ends[chunk]
    placed = [None] * chunks
    for chunk, at in enumerate(places):
        placed[at] = sent[chunk]
    for pair in range(chunks // 2):
        both = jnp.concatenate(placed[2 * pair : 2 * pair + 2], axis=0)
        out_ref[pair * 2 * BLOCK : (pair + 1) * 2 * BLOCK, :] = both.astype(BF16)


def output_kernel(
    length,
    carried_ref,
    conv_ref,
    back_ref,
    ahead_ref,
    behind_ref,
    fade_ref,
    key_ref,
    value_ref,
    out_grad_ref,
    log_ref,
    residue_ref,
    query_out,
    key_out,
    value_out,
    residue_out,
    log_out,
):
    width, channels = conv_ref.shape
    blocks = width // BLOCK
    rows = carried_ref[...].astype(F32).T
    rows = rows[: LANES // 2] + rows[LANES // 2 :]
    residue_out[...] = rows[2 * POLES : 3 * POLES] * (1.0 / length)
    rates = jnp.exp(log_ref[...]) / length
    log_out[...] = -(residue_ref[...] / length) * rates * rows[3 * POLES :]
    for half in range(channels // LANES):
        here = slice(half * LANES, (half + 1) * LANES)
        total = [conv_ref[block * BLOCK : (block + 1) * BLOCK, here] for block in range(blocks)]
        for pole in range(POLES):
            term = ahead_ref[pole, :, here] * rows[pole : pole + 1, here]
            fade = fade_ref[pole : pole + 1, here]
            for block in range(blocks):
                total[block] = total[block] + term
                term = term * fade
        conv = jnp.concatenate(total, axis=0).T.astype(BF16).astype(F32)
        query_out[here, :] = (out_grad_ref[here, :].astype(F32) * conv).astype(BF16)
        total = [back_ref[block * BLOCK : (block + 1) * BLOCK, here] for block in range(blocks)]
        for pole in range(POLES):
            term = behind_ref[pole, :, here] * rows[POLES + pole : POLES + pole + 1, here]
            fade = fade_ref[pole : pole + 1, here]
            for block in range(blocks - 1, -1, -1):
                total[block] = total[block] + term
                term = term * fade
        back = jnp.concatenate(total, axis=0).T.astype(BF16).astype(F32)
        key_out[here, :] = (back * value_ref[here, :].astype(F32)).astype(BF16)
        value_out[here, :] = (back * key_ref[here, :].astype(F32)).astype(BF16)


def member_order(chunks):
    return [(place + chunks // 2) % chunks for place in range(chunks)]


def on_device(query, key_gate, value_in, grad_output, residue, log_rate):
    chunks = lax.axis_size("ctx")
    channels, width = query.shape
    length = width * chunks
    struct = jax.ShapeDtypeStruct
    in_vmem = pl.BlockSpec(memory_space=pltpu.VMEM)
    turned = [pltpu.VMEM((width, channels), F32)] * 2
    held = [pltpu.VMEM((channels, width), BF16)] * 4 + [pltpu.VMEM((POLES, channels), F32)] * 2
    params = pltpu.CompilerParams(vmem_limit_bytes=32 * MIB)
    poles = (log_rate.T, residue.T)
    sources = [pltpu.with_memory_space_constraint(x, pltpu.HBM) for x in (key_gate, value_in, query, grad_output, *poles)]
    in_hbm = pl.BlockSpec(memory_space=pltpu.HBM)
    sent = struct((channels, LANES), BF16)
    per_chunk = (chunks, channels // chunks, LANES)
    order = member_order(chunks)
    places = [order.index(member) for member in range(chunks)]

    def exchange(table):
        table = lax.all_to_all(
            table.reshape(per_chunk), "ctx", split_axis=0, concat_axis=0, axis_index_groups=[order], tiled=True
        )
        return table.reshape(channels, LANES)

    summary = pl.pallas_call(
        functools.partial(summary_kernel, float(length)),
        out_shape=sent,
        in_specs=[in_hbm] * 5,
        out_specs=in_vmem,
        scratch_shapes=[*turned, pltpu.SemaphoreType.DMA((5,)), *held[:5]],
        compiler_params=params,
        name="chunk_summary",
    )(*sources[:5])
    parts = exchange(summary)
    index = lax.axis_index("ctx").astype(jnp.int32).reshape(1)
    conv, back, ahead, behind, fade, chunk_fade = pl.pallas_call(
        functools.partial(local_kernel, float(length), places),
        out_shape=(
            struct((width, channels), F32),
            struct((width, channels), F32),
            struct((POLES, BLOCK, channels), F32),
            struct((POLES, BLOCK, channels), F32),
            struct((POLES, channels), F32),
            struct((BLOCK, LANES), F32),
        ),
        in_specs=[pl.BlockSpec(memory_space=pltpu.SMEM)] + [in_hbm] * 6,
        out_specs=[in_vmem] * 6,
        scratch_shapes=[*turned, pltpu.VMEM((channels, LANES), F32), pltpu.SemaphoreType.DMA((6,)), *held],
        compiler_params=params,
        name="local_part",
        cost_estimate=pl.CostEstimate(flops=20_000_000, bytes_accessed=1_500_000, transcendentals=0),
    )(index, *sources)
    carried = pl.pallas_call(
        functools.partial(prefix_kernel, float(width), places),
        out_shape=sent,
        in_specs=[in_vmem] * 2,
        out_specs=in_vmem,
        compiler_params=params,
        name="chunk_prefix",
    )(parts, chunk_fade)
    carried = exchange(carried)
    gate_out = struct((channels, width), BF16)
    pole_out = struct((POLES, channels), F32)
    outs = pl.pallas_call(
        functools.partial(output_kernel, float(length)),
        out_shape=(gate_out, gate_out, gate_out, pole_out, pole_out),
        in_specs=[in_vmem] * 11,
        out_specs=[in_vmem] * 5,
        compiler_params=params,
        name="outputs",
    )(carried, conv, back, ahead, behind, fade, key_gate, value_in, grad_output, *poles)
    return (*outs[:3], outs[3].T, outs[4].T)


def solution(mesh):
    both = P("ch", "ctx")
    rows = P("ch", None)
    return jax.shard_map(
        on_device,
        mesh=mesh,
        in_specs=(both, both, both, both, rows, rows),
        out_specs=(both, both, both, rows, rows),
        check_vma=False,
    )
```

```python
import functools

import jax
import jax.numpy as jnp
from jax import lax
from jax.experimental import pallas as pl
from jax.experimental.pallas import tpu as pltpu
from jax.sharding import PartitionSpec as P

F32 = jnp.float32
BF16 = jnp.bfloat16
POLES = 16
BLOCK = 8
LANES = 128
NEAR = 4
EARLY = 8
MIB = 1024 * 1024


def gated(left_ref, right_ref):
    product = (left_ref[...].astype(F32) * right_ref[...].astype(F32)).astype(BF16)
    return product.astype(F32).T


def crossed(first, second):
    left = lax.broadcasted_iota(jnp.int32, first.shape, 1) < LANES // 2
    return (
        jnp.where(left, first, pltpu.roll(second, LANES // 2, 1)),
        jnp.where(left, pltpu.roll(first, LANES // 2, 1), second),
    )


def unpacked(block):
    low = pltpu.roll(block, LANES // 2, 1)
    return [half[at * POLES : (at + 1) * POLES] for half in (block, low) for at in range(3)]


def joined(parts, fade, width):
    zero = jnp.zeros(fade.shape, F32)
    state, moment, res, rate = zero, zero, zero, zero
    ahead, behind = [], []
    for end, start, end_moment, start_moment, part_res, part_rate in parts:
        ahead.append(state)
        res = res + part_res + start * state
        rate = rate + part_rate + start_moment * state + start * moment
        moment = fade * (moment + width * state) + end_moment
        state = fade * state + end
    back, back_moment = zero, zero
    for _, start, _, start_moment, _, _ in parts[::-1]:
        behind.append(back)
        back_moment = fade * (back_moment + width * back) + start_moment
        back = fade * back + start
    return (state, back, moment, back_moment, res, rate), ahead, behind[::-1]


def own_rates(length, near, index, log_ref):
    block = near - 1 - lax.rem(index, near)
    logs = jnp.where(block >= 2, log_ref[:, LANES:], log_ref[:, :LANES])
    logs = jnp.where(lax.rem(block, 2) == 1, pltpu.roll(logs, LANES // 2, 1), logs)
    return jnp.exp(logs) / length


def load_gates(sources, held, sems, mixed, grad):
    copies = [pltpu.make_async_copy(src, dst, sems.at[n]) for n, (src, dst) in enumerate(zip(sources, held))]
    for copy in copies:
        copy.start()
    copies[0].wait()
    copies[1].wait()
    mixed[...] = gated(held[0], held[1])
    copies[2].wait()
    copies[3].wait()
    grad[...] = gated(held[2], held[3])
    for copy in copies[4:]:
        copy.wait()


def summary_kernel(length, index_ref, *refs):
    sources, out_ref, held, (mixed, grad, sems) = refs[:6], refs[6], refs[7:13], refs[13:]
    load_gates(sources, held, sems, mixed, grad)
    log_ref = held[4]
    width, channels = mixed.shape
    decay = jnp.exp(-(jnp.exp(log_ref[...]) / length))
    zero = jnp.zeros((POLES, channels), F32)

    def step(block, carry):
        state, moment, res, rate, back, back_moment = carry
        first = block * BLOCK
        for row in range(BLOCK):
            mixed_row = mixed[pl.ds(first + row, 1), :]
            grad_row = grad[pl.ds(first + row, 1), :]
            late_row = grad[pl.ds(width - 1 - first - row, 1), :]
            faded = decay * state
            state = faded + mixed_row
            moment = decay * moment + faded
            res = res + grad_row * state
            rate = rate + grad_row * moment
            faded = decay * back
            back = faded + late_row
            back_moment = decay * back_moment + faded
        return state, moment, res, rate, back, back_moment

    state, moment, res, rate, back, back_moment = lax.fori_loop(0, width // BLOCK, step, (zero,) * 6)
    last = decay * state
    last_moment = decay * moment + last
    top = jnp.concatenate([last, back, last_moment], axis=0)
    low = jnp.concatenate([back_moment, res, rate], axis=0)
    rows = top.shape[0]
    for half in range(channels // LANES):
        here = slice(half * LANES, (half + 1) * LANES)
        pair = crossed(top[:, here], low[:, here])
        for side in range(2):
            block = 2 * half + side
            out_ref[block * rows : (block + 1) * rows, :] = pair[side]


def local_part(length, mixed, grad, log_ref, residue_ref, conv_ref, back_ref, ahead_ref, behind_ref, fade_ref):
    width, channels = mixed.shape
    rates = jnp.exp(log_ref[...]) / length
    decay = jnp.exp(-rates)
    weight = residue_ref[...] * (length**-0.5)
    zero = jnp.zeros((POLES, channels), F32)

    def step(block, carry):
        state, back = carry
        first = pl.multiple_of(block * BLOCK, BLOCK)
        last = pl.multiple_of(width - BLOCK - block * BLOCK, BLOCK)
        ahead, behind = [], []
        for row in range(BLOCK):
            state = decay * state + mixed[pl.ds(first + row, 1), :]
            ahead.append(jnp.sum(weight * state, axis=0, keepdims=True))
            back = decay * back + grad[pl.ds(last + BLOCK - 1 - row, 1), :]
            behind.append(jnp.sum(weight * back, axis=0, keepdims=True))
        conv_ref[pl.ds(first, BLOCK), :] = jnp.concatenate(ahead, axis=0)
        back_ref[pl.ds(last, BLOCK), :] = jnp.concatenate(behind[::-1], axis=0)
        return state, back

    lax.fori_loop(0, width // BLOCK, step, (zero, zero))
    steps = lax.broadcasted_iota(jnp.int32, (BLOCK, channels), 0).astype(F32)
    for pole in range(POLES):
        rate = rates[pole : pole + 1]
        scale = weight[pole : pole + 1]
        ahead_ref[pole] = scale * jnp.exp(-(rate * steps))
        behind_ref[pole] = scale * jnp.exp(-(rate * (BLOCK - steps)))
    fade_ref[...] = jnp.exp(-(rates * BLOCK))


def group_kernel(length, width, near, index_ref, parts_ref, mixed, grad, log_ref, residue_ref, out_ref, *tables):
    rows = 3 * POLES

    @pl.when(index_ref[0] < EARLY)
    def _():
        local_part(length, mixed, grad, log_ref, residue_ref, *tables)

    fade = jnp.exp(-(own_rates(length, near, index_ref[0], log_ref) * width))
    parts = [unpacked(parts_ref[at * rows : (at + 1) * rows, :]) for at in range(near - 1, -1, -1)]
    whole, _, _ = joined(parts, fade, width)
    end, start, end_moment, start_moment, res, rate = whole
    top = jnp.concatenate([end, start, end_moment], axis=0)
    low = jnp.concatenate([start_moment, res, rate], axis=0)
    sent = crossed(top, low)[0].astype(BF16)
    for at in range(out_ref.shape[0] // rows):
        out_ref[at * rows : (at + 1) * rows, :] = sent


def total_kernel(length, width, near, far_order, index_ref, parts_ref, groups_ref, log_ref, out_ref):
    rows = 3 * POLES
    index = index_ref[0]
    group = lax.div(index, near)
    rates = own_rates(length, near, index, log_ref)
    fade = jnp.exp(-(rates * width))
    groups = [None] * len(far_order)
    for at, member in enumerate(far_order):
        groups[member] = unpacked(groups_ref[at * rows : (at + 1) * rows, :].astype(F32))
    whole, ahead, behind = joined(groups, jnp.exp(-(rates * (width * near))), width * near)
    state, back = ahead[0], behind[0]
    for member in range(1, len(groups)):
        state = jnp.where(group == member, ahead[member], state)
        back = jnp.where(group == member, behind[member], back)
    states, backs = [], []
    for chunk in range(near):
        block = parts_ref[(near - 1 - chunk) * rows : (near - chunk) * rows, :]
        states.append(state)
        state = fade * state + block[:POLES]
    for chunk in range(near - 1, -1, -1):
        block = parts_ref[(near - 1 - chunk) * rows : (near - chunk) * rows, :]
        backs.append(back)
        back = fade * back + block[POLES : 2 * POLES]
    totals = jnp.concatenate(whole[4:], axis=0)
    rows = 2 * POLES
    for at in range(near):
        entering = jnp.concatenate([states[near - 1 - at], backs[at]], axis=0)
        out_ref[at * rows : (at + 1) * rows, :] = crossed(entering, totals)[0]


def output_kernel(length, index_ref, carried_ref, *refs):
    early, (key_ref, value_ref, out_grad_ref, log_ref, residue_ref, mixed, grad), outs, late = (
        refs[:5],
        refs[5:12],
        refs[12:17],
        refs[17:],
    )
    residue_out, log_out = outs[3:]
    channels = residue_ref.shape[1]
    rates = jnp.exp(log_ref[...]) / length
    rate_scale = -(residue_ref[...] / length) * rates
    size = 2 * POLES
    states = []
    for half in range(channels // LANES):
        here = slice(half * LANES, (half + 1) * LANES)
        first, second = (carried_ref[at * size : (at + 1) * size, :] for at in (2 * half, 2 * half + 1))
        entering, totals = crossed(first, second)
        states.append(entering)
        residue_out[:, here] = totals[:POLES] * (1.0 / length)
        log_out[:, here] = rate_scale[:, here] * totals[POLES:]

    @pl.when(index_ref[0] < EARLY)
    def _():
        gate_gradients(states, early, key_ref, value_ref, out_grad_ref, *outs[:3])

    @pl.when(index_ref[0] >= EARLY)
    def _():
        local_part(length, mixed, grad, log_ref, residue_ref, *late)
        gate_gradients(states, late, key_ref, value_ref, out_grad_ref, *outs[:3])


def gate_gradients(states, tables, key_ref, value_ref, out_grad_ref, query_out, key_out, value_out):
    conv_ref, back_ref, ahead_ref, behind_ref, fade_ref = tables
    blocks = conv_ref.shape[0] // BLOCK
    for half, entering in enumerate(states):
        here = slice(half * LANES, (half + 1) * LANES)
        total = [conv_ref[block * BLOCK : (block + 1) * BLOCK, here] for block in range(blocks)]
        for pole in range(POLES):
            term = ahead_ref[pole, :, here] * entering[pole : pole + 1]
            fade = fade_ref[pole : pole + 1, here]
            for block in range(blocks):
                total[block] = total[block] + term
                term = term * fade
        conv = jnp.concatenate(total, axis=0).T.astype(BF16).astype(F32)
        query_out[here, :] = (out_grad_ref[here, :].astype(F32) * conv).astype(BF16)
        total = [back_ref[block * BLOCK : (block + 1) * BLOCK, here] for block in range(blocks)]
        for pole in range(POLES):
            term = behind_ref[pole, :, here] * entering[POLES + pole : POLES + pole + 1]
            fade = fade_ref[pole : pole + 1, here]
            for block in range(blocks - 1, -1, -1):
                total[block] = total[block] + term
                term = term * fade
        back = jnp.concatenate(total, axis=0).T.astype(BF16).astype(F32)
        key_out[here, :] = (back * value_ref[here, :].astype(F32)).astype(BF16)
        value_out[here, :] = (back * key_ref[here, :].astype(F32)).astype(BF16)


def on_device(query, key_gate, value_in, grad_output, residue, log_rate):
    chunks = lax.axis_size("ctx")
    channels, width = query.shape
    length = width * chunks
    struct = jax.ShapeDtypeStruct
    in_vmem = pl.BlockSpec(memory_space=pltpu.VMEM)
    in_smem = pl.BlockSpec(memory_space=pltpu.SMEM)
    in_hbm = pl.BlockSpec(memory_space=pltpu.HBM)
    params = pltpu.CompilerParams(vmem_limit_bytes=32 * MIB)
    gate, pole = struct((channels, width), BF16), struct((POLES, channels), F32)
    turned = struct((width, channels), F32)
    spread = struct((POLES, BLOCK, channels), F32)
    sources = [key_gate, value_in, query, grad_output, log_rate.T, residue.T]
    sources = [pltpu.with_memory_space_constraint(source, pltpu.HBM) for source in sources]
    tables = (turned, turned, spread, spread, pole)
    index = lax.axis_index("ctx").astype(jnp.int32).reshape(1)
    near, far = NEAR, chunks // NEAR
    rows = 3 * POLES
    far_order = [(5 * far // 8 - place) % far for place in range(far)]
    near_groups = [[group * near + near - 1 - place for place in range(near)] for group in range(far)]
    far_groups = [[group * near + member for group in far_order] for member in range(near)]

    def exchange(table, groups):
        members = len(groups[0])
        shape = table.shape
        table = table.reshape(members, shape[0] // members, LANES)
        table = lax.all_to_all(table, "ctx", split_axis=0, concat_axis=0, axis_index_groups=groups, tiled=True)
        return table.reshape(shape)

    summary, key_gate, value_in, _, grad_output, logs, residues, mixed, grad = pl.pallas_call(
        functools.partial(summary_kernel, float(length)),
        out_shape=(struct((near * rows, LANES), F32), gate, gate, gate, gate, pole, pole, turned, turned),
        in_specs=[in_smem] + [in_hbm] * 6,
        out_specs=[in_vmem] * 9,
        scratch_shapes=[pltpu.SemaphoreType.DMA((6,))],
        compiler_params=params,
        name="chunk_summary",
    )(index, *sources)
    parts = exchange(summary, near_groups)
    group, *early = pl.pallas_call(
        functools.partial(group_kernel, float(length), float(width), near),
        out_shape=(struct((far * rows, LANES), BF16), *tables),
        in_specs=[in_smem] + [in_vmem] * 5,
        out_specs=[in_vmem] * 6,
        compiler_params=params,
        name="group_summary",
    )(index, parts, mixed, grad, logs, residues)
    groups = exchange(group, far_groups)
    carried = pl.pallas_call(
        functools.partial(total_kernel, float(length), float(width), near, far_order),
        out_shape=struct((near * 2 * POLES, LANES), F32),
        in_specs=[in_smem, in_vmem, in_vmem, in_vmem],
        out_specs=in_vmem,
        compiler_params=params,
        name="totals",
    )(index, parts, groups, logs)
    carried = exchange(carried, near_groups)
    outs = pl.pallas_call(
        functools.partial(output_kernel, float(length)),
        out_shape=(gate, gate, gate, pole, pole),
        in_specs=[in_smem] + [in_vmem] * 13,
        out_specs=[in_vmem] * 5,
        scratch_shapes=[pltpu.VMEM(table.shape, table.dtype) for table in tables],
        compiler_params=params,
        name="outputs",
    )(index, carried, *early, key_gate, value_in, grad_output, logs, residues, mixed, grad)
    return (*outs[:3], outs[3].T, outs[4].T)


def solution(mesh):
    both = P("ch", "ctx")
    rows = P("ch", None)
    return jax.shard_map(
        on_device,
        mesh=mesh,
        in_specs=(both, both, both, both, rows, rows),
        out_specs=(both, both, both, rows, rows),
        check_vma=False,
    )
```

```python
import functools

import jax
import jax.numpy as jnp
from jax import lax
from jax.experimental import pallas as pl
from jax.experimental.pallas import tpu as pltpu
from jax.sharding import PartitionSpec as P

F32 = jnp.float32
BF16 = jnp.bfloat16
POLES = 16
BLOCK = 8
LANES = 128
NEAR = 4
FLIP = 3
STEPS = 32
EARLY = 8
MIB = 1024 * 1024


def gated(left_ref, right_ref):
    product = (left_ref[...].astype(F32) * right_ref[...].astype(F32)).astype(BF16)
    return product.astype(F32).T


def crossed(first, second):
    left = lax.broadcasted_iota(jnp.int32, first.shape, 1) < LANES // 2
    return (
        jnp.where(left, first, pltpu.roll(second, LANES // 2, 1)),
        jnp.where(left, pltpu.roll(first, LANES // 2, 1), second),
    )


def unpacked(block):
    low = pltpu.roll(block, LANES // 2, 1)
    return [half[at * POLES : (at + 1) * POLES] for half in (block, low) for at in range(3)]


def joined(parts, fade, width):
    zero = jnp.zeros(fade.shape, F32)
    state, moment, res, rate = zero, zero, zero, zero
    ahead, behind = [], []
    for end, start, end_moment, start_moment, part_res, part_rate in parts:
        ahead.append(state)
        res = res + part_res + start * state
        rate = rate + part_rate + start_moment * state + start * moment
        moment = fade * (moment + width * state) + end_moment
        state = fade * state + end
    back, back_moment = zero, zero
    for _, start, _, start_moment, _, _ in parts[::-1]:
        behind.append(back)
        back_moment = fade * (back_moment + width * back) + start_moment
        back = fade * back + start
    return (state, back, moment, back_moment, res, rate), ahead, behind[::-1]


def own_rates(length, near, index, log_ref):
    block = jnp.bitwise_xor(lax.rem(index, near), FLIP)
    logs = jnp.where(block >= 2, log_ref[:, LANES:], log_ref[:, :LANES])
    logs = jnp.where(lax.rem(block, 2) == 1, pltpu.roll(logs, LANES // 2, 1), logs)
    return jnp.exp(logs) / length


def load_gates(sources, held, sems, mixed, grad):
    copies = [pltpu.make_async_copy(src, dst, sems.at[n]) for n, (src, dst) in enumerate(zip(sources, held))]
    for copy in copies:
        copy.start()
    copies[0].wait()
    copies[1].wait()
    mixed[...] = gated(held[0], held[1])
    copies[2].wait()
    copies[3].wait()
    grad[...] = gated(held[2], held[3])
    for copy in copies[4:]:
        copy.wait()


def summary_kernel(length, index_ref, *refs):
    sources, out_ref, held, (mixed, grad, query_ref, sems) = refs[:6], refs[6], refs[7:12], refs[12:]
    held = (*held[:2], query_ref, *held[2:])
    load_gates(sources, held, sems, mixed, grad)
    log_ref = held[4]
    width, channels = mixed.shape
    decay = jnp.exp(-(jnp.exp(log_ref[...]) / length))
    zero = jnp.zeros((POLES, channels), F32)

    def step(block, carry):
        state, moment, res, rate, back, back_moment = carry
        first = block * STEPS
        for row in range(STEPS):
            mixed_row = mixed[pl.ds(first + row, 1), :]
            grad_row = grad[pl.ds(first + row, 1), :]
            late_row = grad[pl.ds(width - 1 - first - row, 1), :]
            faded = decay * state
            state = faded + mixed_row
            moment = decay * moment + faded
            res = res + grad_row * state
            rate = rate + grad_row * moment
            faded = decay * back
            back = faded + late_row
            back_moment = decay * back_moment + faded
        return state, moment, res, rate, back, back_moment

    state, moment, res, rate, back, back_moment = lax.fori_loop(0, width // STEPS, step, (zero,) * 6)
    last = decay * state
    last_moment = decay * moment + last
    top = jnp.concatenate([last, back, last_moment], axis=0)
    low = jnp.concatenate([back_moment, res, rate], axis=0)
    rows = top.shape[0]
    for half in range(channels // LANES):
        here = slice(half * LANES, (half + 1) * LANES)
        pair = crossed(top[:, here], low[:, here])
        for side in range(2):
            block = 2 * half + side
            out_ref[block * rows : (block + 1) * rows, :] = pair[side]


def local_part(length, mixed, grad, log_ref, residue_ref, conv_ref, back_ref, ahead_ref, behind_ref, fade_ref):
    width, channels = mixed.shape
    rates = jnp.exp(log_ref[...]) / length
    decay = jnp.exp(-rates)
    weight = residue_ref[...] * (length**-0.5)
    zero = jnp.zeros((POLES, channels), F32)

    def step(block, carry):
        state, back = carry
        first = pl.multiple_of(block * BLOCK, BLOCK)
        last = pl.multiple_of(width - BLOCK - block * BLOCK, BLOCK)
        ahead, behind = [], []
        for row in range(BLOCK):
            state = decay * state + mixed[pl.ds(first + row, 1), :]
            ahead.append(jnp.sum(weight * state, axis=0, keepdims=True))
            back = decay * back + grad[pl.ds(last + BLOCK - 1 - row, 1), :]
            behind.append(jnp.sum(weight * back, axis=0, keepdims=True))
        conv_ref[pl.ds(first, BLOCK), :] = jnp.concatenate(ahead, axis=0)
        back_ref[pl.ds(last, BLOCK), :] = jnp.concatenate(behind[::-1], axis=0)
        return state, back

    lax.fori_loop(0, width // BLOCK, step, (zero, zero))
    steps = lax.broadcasted_iota(jnp.int32, (BLOCK, channels), 0).astype(F32)
    for pole in range(POLES):
        rate = rates[pole : pole + 1]
        scale = weight[pole : pole + 1]
        ahead_ref[pole] = scale * jnp.exp(-(rate * steps))
        behind_ref[pole] = scale * jnp.exp(-(rate * (BLOCK - steps)))
    fade_ref[...] = jnp.exp(-(rates * BLOCK))


def group_kernel(length, width, near, index_ref, parts_ref, mixed, grad, log_ref, residue_ref, out_ref, *tables):
    rows = 3 * POLES

    @pl.when(index_ref[0] < EARLY)
    def _():
        local_part(length, mixed, grad, log_ref, residue_ref, *tables)

    fade = jnp.exp(-(own_rates(length, near, index_ref[0], log_ref) * width))
    places = [chunk ^ FLIP for chunk in range(near)]
    parts = [unpacked(parts_ref[at * rows : (at + 1) * rows, :]) for at in places]
    whole, _, _ = joined(parts, fade, width)
    end, start, end_moment, start_moment, res, rate = whole
    top = jnp.concatenate([end, start, end_moment], axis=0)
    low = jnp.concatenate([start_moment, res, rate], axis=0)
    sent = crossed(top, low)[0].astype(BF16)
    for at in range(out_ref.shape[0] // rows):
        out_ref[at * rows : (at + 1) * rows, :] = sent


def total_kernel(length, width, near, far_order, index_ref, parts_ref, groups_ref, log_ref, out_ref):
    rows = 3 * POLES
    index = index_ref[0]
    group = lax.div(index, near)
    rates = own_rates(length, near, index, log_ref)
    fade = jnp.exp(-(rates * width))
    groups = [None] * len(far_order)
    for at, member in enumerate(far_order):
        groups[member] = unpacked(groups_ref[at * rows : (at + 1) * rows, :].astype(F32))
    whole, ahead, behind = joined(groups, jnp.exp(-(rates * (width * near))), width * near)
    state, back = ahead[0], behind[0]
    for member in range(1, len(groups)):
        state = jnp.where(group == member, ahead[member], state)
        back = jnp.where(group == member, behind[member], back)
    states, backs = [], []
    for chunk in range(near):
        at = chunk ^ FLIP
        block = parts_ref[at * rows : (at + 1) * rows, :]
        states.append(state)
        state = fade * state + block[:POLES]
    for chunk in range(near - 1, -1, -1):
        at = chunk ^ FLIP
        block = parts_ref[at * rows : (at + 1) * rows, :]
        backs.append(back)
        back = fade * back + block[POLES : 2 * POLES]
    totals = jnp.concatenate(whole[4:], axis=0)
    rows = 2 * POLES
    for at in range(near):
        chunk = at ^ FLIP
        entering = jnp.concatenate([states[chunk], backs[near - 1 - chunk]], axis=0)
        out_ref[at * rows : (at + 1) * rows, :] = crossed(entering, totals)[0]


def output_kernel(length, index_ref, carried_ref, *refs):
    early, (key_ref, value_ref, out_grad_ref, log_ref, residue_ref, mixed, grad), outs, late = (
        refs[:5],
        refs[5:12],
        refs[12:17],
        refs[17:],
    )
    residue_out, log_out = outs[3:]
    channels = residue_ref.shape[1]
    rates = jnp.exp(log_ref[...]) / length
    rate_scale = -(residue_ref[...] / length) * rates
    size = 2 * POLES
    states = []
    for half in range(channels // LANES):
        here = slice(half * LANES, (half + 1) * LANES)
        first, second = (carried_ref[at * size : (at + 1) * size, :] for at in (2 * half, 2 * half + 1))
        entering, totals = crossed(first, second)
        states.append(entering)
        residue_out[:, here] = totals[:POLES] * (1.0 / length)
        log_out[:, here] = rate_scale[:, here] * totals[POLES:]

    @pl.when(index_ref[0] < EARLY)
    def _():
        gate_gradients(states, early, key_ref, value_ref, out_grad_ref, *outs[:3])

    @pl.when(index_ref[0] >= EARLY)
    def _():
        local_part(length, mixed, grad, log_ref, residue_ref, *late)
        gate_gradients(states, late, key_ref, value_ref, out_grad_ref, *outs[:3])


def gate_gradients(states, tables, key_ref, value_ref, out_grad_ref, query_out, key_out, value_out):
    conv_ref, back_ref, ahead_ref, behind_ref, fade_ref = tables
    blocks = conv_ref.shape[0] // BLOCK
    for half, entering in enumerate(states):
        here = slice(half * LANES, (half + 1) * LANES)
        total = [conv_ref[block * BLOCK : (block + 1) * BLOCK, here] for block in range(blocks)]
        for pole in range(POLES):
            term = ahead_ref[pole, :, here] * entering[pole : pole + 1]
            fade = fade_ref[pole : pole + 1, here]
            for block in range(blocks):
                total[block] = total[block] + term
                term = term * fade
        conv = jnp.concatenate(total, axis=0).T.astype(BF16).astype(F32)
        query_out[here, :] = (out_grad_ref[here, :].astype(F32) * conv).astype(BF16)
        total = [back_ref[block * BLOCK : (block + 1) * BLOCK, here] for block in range(blocks)]
        for pole in range(POLES):
            term = behind_ref[pole, :, here] * entering[POLES + pole : POLES + pole + 1]
            fade = fade_ref[pole : pole + 1, here]
            for block in range(blocks - 1, -1, -1):
                total[block] = total[block] + term
                term = term * fade
        back = jnp.concatenate(total, axis=0).T.astype(BF16).astype(F32)
        key_out[here, :] = (back * value_ref[here, :].astype(F32)).astype(BF16)
        value_out[here, :] = (back * key_ref[here, :].astype(F32)).astype(BF16)


def on_device(query, key_gate, value_in, grad_output, residue, log_rate):
    chunks = lax.axis_size("ctx")
    channels, width = query.shape
    length = width * chunks
    struct = jax.ShapeDtypeStruct
    in_vmem = pl.BlockSpec(memory_space=pltpu.VMEM)
    in_smem = pl.BlockSpec(memory_space=pltpu.SMEM)
    in_hbm = pl.BlockSpec(memory_space=pltpu.HBM)
    params = pltpu.CompilerParams(vmem_limit_bytes=32 * MIB)
    gate, pole = struct((channels, width), BF16), struct((POLES, channels), F32)
    turned = struct((width, channels), F32)
    spread = struct((POLES, BLOCK, channels), F32)
    sources = [key_gate, value_in, query, grad_output, log_rate.T, residue.T]
    sources = [pltpu.with_memory_space_constraint(source, pltpu.HBM) for source in sources]
    tables = (turned, turned, spread, spread, pole)
    index = lax.axis_index("ctx").astype(jnp.int32).reshape(1)
    near, far = NEAR, chunks // NEAR
    rows = 3 * POLES
    far_order = [(5 * far // 8 - place) % far for place in range(far)]
    near_groups = [[group * near + (place ^ FLIP) for place in range(near)] for group in range(far)]
    far_groups = [[group * near + member for group in far_order] for member in range(near)]

    def exchange(table, groups):
        members = len(groups[0])
        shape = table.shape
        table = table.reshape(members, shape[0] // members, LANES)
        table = lax.all_to_all(table, "ctx", split_axis=0, concat_axis=0, axis_index_groups=groups, tiled=True)
        return table.reshape(shape)

    summary, key_gate, value_in, grad_output, logs, residues, mixed, grad = pl.pallas_call(
        functools.partial(summary_kernel, float(length)),
        out_shape=(struct((near * rows, LANES), F32), gate, gate, gate, pole, pole, turned, turned),
        in_specs=[in_smem] + [in_hbm] * 6,
        out_specs=[in_vmem] * 8,
        scratch_shapes=[pltpu.VMEM(gate.shape, gate.dtype), pltpu.SemaphoreType.DMA((6,))],
        compiler_params=params,
        name="chunk_summary",
    )(index, *sources)
    parts = exchange(summary, near_groups)
    group, *early = pl.pallas_call(
        functools.partial(group_kernel, float(length), float(width), near),
        out_shape=(struct((far * rows, LANES), BF16), *tables),
        in_specs=[in_smem] + [in_vmem] * 5,
        out_specs=[in_vmem] * 6,
        compiler_params=params,
        name="group_summary",
    )(index, parts, mixed, grad, logs, residues)
    groups = exchange(group, far_groups)
    carried = pl.pallas_call(
        functools.partial(total_kernel, float(length), float(width), near, far_order),
        out_shape=struct((near * 2 * POLES, LANES), F32),
        in_specs=[in_smem, in_vmem, in_vmem, in_vmem],
        out_specs=in_vmem,
        compiler_params=params,
        name="totals",
    )(index, parts, groups, logs)
    carried = exchange(carried, near_groups)
    outs = pl.pallas_call(
        functools.partial(output_kernel, float(length)),
        out_shape=(gate, gate, gate, pole, pole),
        in_specs=[in_smem] + [in_vmem] * 13,
        out_specs=[in_vmem] * 5,
        scratch_shapes=[pltpu.VMEM(table.shape, table.dtype) for table in tables],
        compiler_params=params,
        name="outputs",
    )(index, carried, *early, key_gate, value_in, grad_output, logs, residues, mixed, grad)
    return (*outs[:3], outs[3].T, outs[4].T)


def solution(mesh):
    both = P("ch", "ctx")
    rows = P("ch", None)
    return jax.shard_map(
        on_device,
        mesh=mesh,
        in_specs=(both, both, both, both, rows, rows),
        out_specs=(both, both, both, rows, rows),
        check_vma=False,
    )
```

```python
import functools

import jax
import jax.numpy as jnp
from jax import lax
from jax.experimental import pallas as pl
from jax.experimental.pallas import tpu as pltpu
from jax.sharding import PartitionSpec as P

F32 = jnp.float32
BF16 = jnp.bfloat16
POLES = 16
BLOCK = 8
LANES = 128
NEAR = 4
FLIP = 3
STEPS = 64
EARLY = 8
MIB = 1024 * 1024


def gated(left_ref, right_ref):
    product = (left_ref[...].astype(F32) * right_ref[...].astype(F32)).astype(BF16)
    return product.T.astype(F32)


def crossed(first, second):
    left = lax.broadcasted_iota(jnp.int32, first.shape, 1) < LANES // 2
    return (
        jnp.where(left, first, pltpu.roll(second, LANES // 2, 1)),
        jnp.where(left, pltpu.roll(first, LANES // 2, 1), second),
    )


def unpacked(block):
    low = pltpu.roll(block, LANES // 2, 1)
    return [half[at * POLES : (at + 1) * POLES] for half in (block, low) for at in range(3)]


def joined(parts, fade, width):
    zero = jnp.zeros(fade.shape, F32)
    state, moment, res, rate = zero, zero, zero, zero
    ahead, behind = [], []
    for end, start, end_moment, start_moment, part_res, part_rate in parts:
        ahead.append(state)
        res = res + part_res + start * state
        rate = rate + part_rate + start_moment * state + start * moment
        moment = fade * (moment + width * state) + end_moment
        state = fade * state + end
    back, back_moment = zero, zero
    for _, start, _, start_moment, _, _ in parts[::-1]:
        behind.append(back)
        back_moment = fade * (back_moment + width * back) + start_moment
        back = fade * back + start
    return (state, back, moment, back_moment, res, rate), ahead, behind[::-1]


def own_rates(length, near, index, log_ref):
    block = jnp.bitwise_xor(lax.rem(index, near), FLIP)
    logs = jnp.where(block >= 2, log_ref[:, LANES:], log_ref[:, :LANES])
    logs = jnp.where(lax.rem(block, 2) == 1, pltpu.roll(logs, LANES // 2, 1), logs)
    return jnp.exp(logs) / length


def load_gates(sources, held, sems, mixed, grad):
    copies = [pltpu.make_async_copy(src, dst, sems.at[n]) for n, (src, dst) in enumerate(zip(sources, held))]
    for copy in copies:
        copy.start()
    copies[0].wait()
    copies[1].wait()
    mixed[...] = gated(held[0], held[1])
    copies[2].wait()
    copies[3].wait()
    grad[...] = gated(held[2], held[3])
    for copy in copies[4:]:
        copy.wait()


def summary_kernel(length, index_ref, *refs):
    sources, out_ref, held, (mixed, grad, query_ref, sems) = refs[:6], refs[6], refs[7:12], refs[12:]
    held = (*held[:2], query_ref, *held[2:])
    load_gates(sources, held, sems, mixed, grad)
    log_ref = held[4]
    width, channels = mixed.shape
    decay = jnp.exp(-(jnp.exp(log_ref[...]) / length))
    zero = jnp.zeros((POLES, channels), F32)

    def step(block, carry):
        state, moment, res, rate, back, back_moment = carry
        first = block * STEPS
        for row in range(STEPS):
            mixed_row = mixed[pl.ds(first + row, 1), :]
            grad_row = grad[pl.ds(first + row, 1), :]
            late_row = grad[pl.ds(width - 1 - first - row, 1), :]
            faded = decay * state
            state = faded + mixed_row
            moment = decay * moment + faded
            res = res + grad_row * state
            rate = rate + grad_row * moment
            faded = decay * back
            back = faded + late_row
            back_moment = decay * back_moment + faded
        return state, moment, res, rate, back, back_moment

    state, moment, res, rate, back, back_moment = lax.fori_loop(0, width // STEPS, step, (zero,) * 6)
    last = decay * state
    last_moment = decay * moment + last
    top = jnp.concatenate([last, back, last_moment], axis=0)
    low = jnp.concatenate([back_moment, res, rate], axis=0)
    rows = top.shape[0]
    for half in range(channels // LANES):
        here = slice(half * LANES, (half + 1) * LANES)
        pair = crossed(top[:, here], low[:, here])
        for side in range(2):
            block = 2 * half + side
            out_ref[block * rows : (block + 1) * rows, :] = pair[side].astype(BF16)


def local_part(length, mixed, grad, log_ref, residue_ref, conv_ref, back_ref, ahead_ref, behind_ref, fade_ref):
    width, channels = mixed.shape
    rates = jnp.exp(log_ref[...]) / length
    decay = jnp.exp(-rates)
    weight = residue_ref[...] * (length**-0.5)
    zero = jnp.zeros((POLES, channels), F32)

    def step(block, carry):
        state, back = carry
        first = pl.multiple_of(block * BLOCK, BLOCK)
        last = pl.multiple_of(width - BLOCK - block * BLOCK, BLOCK)
        ahead, behind = [], []
        for row in range(BLOCK):
            state = decay * state + mixed[pl.ds(first + row, 1), :]
            ahead.append(jnp.sum(weight * state, axis=0, keepdims=True))
            back = decay * back + grad[pl.ds(last + BLOCK - 1 - row, 1), :]
            behind.append(jnp.sum(weight * back, axis=0, keepdims=True))
        conv_ref[pl.ds(first, BLOCK), :] = jnp.concatenate(ahead, axis=0)
        back_ref[pl.ds(last, BLOCK), :] = jnp.concatenate(behind[::-1], axis=0)
        return state, back

    lax.fori_loop(0, width // BLOCK, step, (zero, zero))
    steps = lax.broadcasted_iota(jnp.int32, (BLOCK, channels), 0).astype(F32)
    for pole in range(POLES):
        rate = rates[pole : pole + 1]
        scale = weight[pole : pole + 1]
        ahead_ref[pole] = scale * jnp.exp(-(rate * steps))
        behind_ref[pole] = scale * jnp.exp(-(rate * (BLOCK - steps)))
    fade_ref[...] = jnp.exp(-(rates * BLOCK))


def group_kernel(length, width, near, index_ref, parts_ref, mixed, grad, log_ref, residue_ref, out_ref, *tables):
    rows = 3 * POLES

    @pl.when(index_ref[0] < EARLY)
    def _():
        local_part(length, mixed, grad, log_ref, residue_ref, *tables)

    fade = jnp.exp(-(own_rates(length, near, index_ref[0], log_ref) * width))
    places = [chunk ^ FLIP for chunk in range(near)]
    parts = [unpacked(parts_ref[at * rows : (at + 1) * rows, :].astype(F32)) for at in places]
    whole, _, _ = joined(parts, fade, width)
    end, start, end_moment, start_moment, res, rate = whole
    top = jnp.concatenate([end, start, end_moment], axis=0)
    low = jnp.concatenate([start_moment, res, rate], axis=0)
    sent = crossed(top, low)[0].astype(BF16)
    for at in range(out_ref.shape[0] // rows):
        out_ref[at * rows : (at + 1) * rows, :] = sent


def total_kernel(length, width, near, far_order, index_ref, parts_ref, groups_ref, log_ref, out_ref):
    rows = 3 * POLES
    index = index_ref[0]
    group = lax.div(index, near)
    rates = own_rates(length, near, index, log_ref)
    fade = jnp.exp(-(rates * width))
    groups = [None] * len(far_order)
    for at, member in enumerate(far_order):
        groups[member] = unpacked(groups_ref[at * rows : (at + 1) * rows, :].astype(F32))
    whole, ahead, behind = joined(groups, jnp.exp(-(rates * (width * near))), width * near)
    state, back = ahead[0], behind[0]
    for member in range(1, len(groups)):
        state = jnp.where(group == member, ahead[member], state)
        back = jnp.where(group == member, behind[member], back)
    states, backs = [], []
    for chunk in range(near):
        at = chunk ^ FLIP
        block = parts_ref[at * rows : (at + 1) * rows, :].astype(F32)
        states.append(state)
        state = fade * state + block[:POLES]
    for chunk in range(near - 1, -1, -1):
        at = chunk ^ FLIP
        block = parts_ref[at * rows : (at + 1) * rows, :].astype(F32)
        backs.append(back)
        back = fade * back + block[POLES : 2 * POLES]
    totals = jnp.concatenate(whole[4:], axis=0)
    rows = 2 * POLES
    for at in range(near):
        chunk = at ^ FLIP
        entering = jnp.concatenate([states[chunk], backs[near - 1 - chunk]], axis=0)
        out_ref[at * rows : (at + 1) * rows, :] = crossed(entering, totals)[0].astype(BF16)


def output_kernel(length, index_ref, carried_ref, *refs):
    early, (key_ref, value_ref, out_grad_ref, log_ref, residue_ref, mixed, grad), outs, late = (
        refs[:5],
        refs[5:12],
        refs[12:17],
        refs[17:],
    )
    residue_out, log_out = outs[3:]
    channels = residue_ref.shape[1]
    rates = jnp.exp(log_ref[...]) / length
    rate_scale = -(residue_ref[...] / length) * rates
    size = 2 * POLES
    states = []
    for half in range(channels // LANES):
        here = slice(half * LANES, (half + 1) * LANES)
        first, second = (carried_ref[at * size : (at + 1) * size, :].astype(F32) for at in (2 * half, 2 * half + 1))
        entering, totals = crossed(first, second)
        states.append(entering)
        residue_out[:, here] = totals[:POLES] * (1.0 / length)
        log_out[:, here] = rate_scale[:, here] * totals[POLES:]

    @pl.when(index_ref[0] < EARLY)
    def _():
        gate_gradients(states, early, key_ref, value_ref, out_grad_ref, *outs[:3])

    @pl.when(index_ref[0] >= EARLY)
    def _():
        local_part(length, mixed, grad, log_ref, residue_ref, *late)
        gate_gradients(states, late, key_ref, value_ref, out_grad_ref, *outs[:3])


def gate_gradients(states, tables, key_ref, value_ref, out_grad_ref, query_out, key_out, value_out):
    conv_ref, back_ref, ahead_ref, behind_ref, fade_ref = tables
    blocks = conv_ref.shape[0] // BLOCK
    for half, entering in enumerate(states):
        here = slice(half * LANES, (half + 1) * LANES)
        total = [conv_ref[block * BLOCK : (block + 1) * BLOCK, here] for block in range(blocks)]
        for pole in range(POLES):
            term = ahead_ref[pole, :, here] * entering[pole : pole + 1]
            fade = fade_ref[pole : pole + 1, here]
            for block in range(blocks):
                total[block] = total[block] + term
                term = term * fade
        conv = jnp.concatenate(total, axis=0).astype(BF16).T.astype(F32)
        query_out[here, :] = (out_grad_ref[here, :].astype(F32) * conv).astype(BF16)
        total = [back_ref[block * BLOCK : (block + 1) * BLOCK, here] for block in range(blocks)]
        for pole in range(POLES):
            term = behind_ref[pole, :, here] * entering[POLES + pole : POLES + pole + 1]
            fade = fade_ref[pole : pole + 1, here]
            for block in range(blocks - 1, -1, -1):
                total[block] = total[block] + term
                term = term * fade
        back = jnp.concatenate(total, axis=0).astype(BF16).T.astype(F32)
        key_out[here, :] = (back * value_ref[here, :].astype(F32)).astype(BF16)
        value_out[here, :] = (back * key_ref[here, :].astype(F32)).astype(BF16)


def on_device(query, key_gate, value_in, grad_output, residue, log_rate):
    chunks = lax.axis_size("ctx")
    channels, width = query.shape
    length = width * chunks
    struct = jax.ShapeDtypeStruct
    in_vmem = pl.BlockSpec(memory_space=pltpu.VMEM)
    in_smem = pl.BlockSpec(memory_space=pltpu.SMEM)
    in_hbm = pl.BlockSpec(memory_space=pltpu.HBM)
    params = pltpu.CompilerParams(vmem_limit_bytes=32 * MIB)
    gate, pole = struct((channels, width), BF16), struct((POLES, channels), F32)
    turned = struct((width, channels), F32)
    spread = struct((POLES, BLOCK, channels), F32)
    sources = [key_gate, value_in, query, grad_output, log_rate.T, residue.T]
    sources = [pltpu.with_memory_space_constraint(source, pltpu.HBM) for source in sources]
    tables = (turned, turned, spread, spread, pole)
    index = lax.axis_index("ctx").astype(jnp.int32).reshape(1)
    near, far = NEAR, chunks // NEAR
    rows = 3 * POLES
    far_order = [(5 * far // 8 - place) % far for place in range(far)]
    near_groups = [[group * near + (place ^ FLIP) for place in range(near)] for group in range(far)]
    far_groups = [[group * near + member for group in far_order] for member in range(near)]

    def exchange(table, groups):
        members = len(groups[0])
        shape = table.shape
        table = table.reshape(members, shape[0] // members, LANES)
        table = lax.all_to_all(table, "ctx", split_axis=0, concat_axis=0, axis_index_groups=groups, tiled=True)
        return table.reshape(shape)

    summary, key_gate, value_in, grad_output, logs, residues, mixed, grad = pl.pallas_call(
        functools.partial(summary_kernel, float(length)),
        out_shape=(struct((near * rows, LANES), BF16), gate, gate, gate, pole, pole, turned, turned),
        in_specs=[in_smem] + [in_hbm] * 6,
        out_specs=[in_vmem] * 8,
        scratch_shapes=[pltpu.VMEM(gate.shape, gate.dtype), pltpu.SemaphoreType.DMA((6,))],
        compiler_params=params,
        name="chunk_summary",
    )(index, *sources)
    parts = exchange(summary, near_groups)
    group, *early = pl.pallas_call(
        functools.partial(group_kernel, float(length), float(width), near),
        out_shape=(struct((far * rows, LANES), BF16), *tables),
        in_specs=[in_smem] + [in_vmem] * 5,
        out_specs=[in_vmem] * 6,
        compiler_params=params,
        name="group_summary",
    )(index, parts, mixed, grad, logs, residues)
    groups = exchange(group, far_groups)
    carried = pl.pallas_call(
        functools.partial(total_kernel, float(length), float(width), near, far_order),
        out_shape=struct((near * 2 * POLES, LANES), BF16),
        in_specs=[in_smem, in_vmem, in_vmem, in_vmem],
        out_specs=in_vmem,
        compiler_params=params,
        name="totals",
    )(index, parts, groups, logs)
    carried = exchange(carried, near_groups)
    outs = pl.pallas_call(
        functools.partial(output_kernel, float(length)),
        out_shape=(gate, gate, gate, pole, pole),
        in_specs=[in_smem] + [in_vmem] * 13,
        out_specs=[in_vmem] * 5,
        scratch_shapes=[pltpu.VMEM(table.shape, table.dtype) for table in tables],
        compiler_params=params,
        name="outputs",
    )(index, carried, *early, key_gate, value_in, grad_output, logs, residues, mixed, grad)
    return (*outs[:3], outs[3].T, outs[4].T)


def solution(mesh):
    both = P("ch", "ctx")
    rows = P("ch", None)
    return jax.shard_map(
        on_device,
        mesh=mesh,
        in_specs=(both, both, both, both, rows, rows),
        out_specs=(both, both, both, rows, rows),
        check_vma=False,
    )
```

```python
import functools

import jax
import jax.numpy as jnp
from jax import lax
from jax.experimental import pallas as pl
from jax.experimental.pallas import tpu as pltpu
from jax.sharding import PartitionSpec as P

F32 = jnp.float32
BF16 = jnp.bfloat16
POLES = 16
BLOCK = 8
LANES = 128
NEAR = 4
FLIP = 3
STEPS = 64
EARLY = 8
MIB = 1024 * 1024


def gated(left_ref, right_ref):
    product = (left_ref[...].astype(F32) * right_ref[...].astype(F32)).astype(BF16)
    return product.T.astype(F32)


def crossed(first, second):
    left = lax.broadcasted_iota(jnp.int32, first.shape, 1) < LANES // 2
    return (
        jnp.where(left, first, pltpu.roll(second, LANES // 2, 1)),
        jnp.where(left, pltpu.roll(first, LANES // 2, 1), second),
    )


def unpacked(block):
    low = pltpu.roll(block, LANES // 2, 1)
    return [half[at * POLES : (at + 1) * POLES] for half in (block, low) for at in range(3)]


def joined(parts, fade, width):
    zero = jnp.zeros(fade.shape, F32)
    state, moment, res, rate = zero, zero, zero, zero
    ahead, behind = [], []
    for end, start, end_moment, start_moment, part_res, part_rate in parts:
        ahead.append(state)
        res = res + part_res + start * state
        rate = rate + part_rate + start_moment * state + start * moment
        moment = fade * (moment + width * state) + end_moment
        state = fade * state + end
    back, back_moment = zero, zero
    for _, start, _, start_moment, _, _ in parts[::-1]:
        behind.append(back)
        back_moment = fade * (back_moment + width * back) + start_moment
        back = fade * back + start
    return (state, back, moment, back_moment, res, rate), ahead, behind[::-1]


def own_rates(length, near, index, log_ref):
    block = jnp.bitwise_xor(lax.rem(index, near), FLIP)
    logs = jnp.where(block >= 2, log_ref[:, LANES:], log_ref[:, :LANES])
    logs = jnp.where(lax.rem(block, 2) == 1, pltpu.roll(logs, LANES // 2, 1), logs)
    return jnp.exp(logs) / length


def load_gates(length, sources, held, sems, mixed, grad):
    pieces = 2
    step = held[0].shape[0] // pieces

    def copies_of(at):
        if at >= 4:
            return [pltpu.make_async_copy(sources[at], held[at], sems.at[at, 0])]
        rows = [pl.ds(piece * step, step) for piece in range(pieces)]
        return [
            pltpu.make_async_copy(sources[at].at[row], held[at].at[row], sems.at[at, piece])
            for piece, row in enumerate(rows)
        ]

    copies = [copies_of(at) for at in range(len(held))]
    for group in (copies[4], *copies[:4], *copies[5:]):
        for copy in group:
            copy.start()

    def arrived(*which):
        for at in which:
            for copy in copies[at]:
                copy.wait()

    arrived(4)
    decay = jnp.exp(-(jnp.exp(held[4][...]) / length))
    arrived(0, 1)
    mixed[...] = gated(held[0], held[1])
    arrived(2, 3)
    grad[...] = gated(held[2], held[3])
    arrived(*range(5, len(held)))
    return decay


def summary_kernel(length, index_ref, *refs):
    sources, out_ref, held, (mixed, grad, query_ref, sems) = refs[:6], refs[6], refs[7:12], refs[12:]
    held = (*held[:2], query_ref, *held[2:])
    decay = load_gates(length, sources, held, sems, mixed, grad)
    width, channels = mixed.shape
    zero = jnp.zeros((POLES, channels), F32)

    def step(block, carry):
        state, moment, res, rate, back, back_moment = carry
        first = block * STEPS
        for row in range(STEPS):
            mixed_row = mixed[pl.ds(first + row, 1), :]
            grad_row = grad[pl.ds(first + row, 1), :]
            late_row = grad[pl.ds(width - 1 - first - row, 1), :]
            faded = decay * state
            state = faded + mixed_row
            moment = decay * moment + faded
            res = res + grad_row * state
            rate = rate + grad_row * moment
            faded = decay * back
            back = faded + late_row
            back_moment = decay * back_moment + faded
        return state, moment, res, rate, back, back_moment

    state, moment, res, rate, back, back_moment = lax.fori_loop(0, width // STEPS, step, (zero,) * 6)
    last = decay * state
    last_moment = decay * moment + last
    top = jnp.concatenate([last, back, last_moment], axis=0)
    low = jnp.concatenate([back_moment, res, rate], axis=0)
    rows = top.shape[0]
    for half in range(channels // LANES):
        here = slice(half * LANES, (half + 1) * LANES)
        pair = crossed(top[:, here], low[:, here])
        for side in range(2):
            block = 2 * half + side
            out_ref[block * rows : (block + 1) * rows, :] = pair[side].astype(BF16)


def local_part(length, mixed, grad, log_ref, residue_ref, conv_ref, back_ref, ahead_ref, behind_ref, fade_ref):
    width, channels = mixed.shape
    rates = jnp.exp(log_ref[...]) / length
    decay = jnp.exp(-rates)
    weight = residue_ref[...] * (length**-0.5)
    zero = jnp.zeros((POLES, channels), F32)

    def step(block, carry):
        state, back = carry
        first = pl.multiple_of(block * BLOCK, BLOCK)
        last = pl.multiple_of(width - BLOCK - block * BLOCK, BLOCK)
        ahead, behind = [], []
        for row in range(BLOCK):
            state = decay * state + mixed[pl.ds(first + row, 1), :]
            ahead.append(jnp.sum(weight * state, axis=0, keepdims=True))
            back = decay * back + grad[pl.ds(last + BLOCK - 1 - row, 1), :]
            behind.append(jnp.sum(weight * back, axis=0, keepdims=True))
        conv_ref[pl.ds(first, BLOCK), :] = jnp.concatenate(ahead, axis=0)
        back_ref[pl.ds(last, BLOCK), :] = jnp.concatenate(behind[::-1], axis=0)
        return state, back

    lax.fori_loop(0, width // BLOCK, step, (zero, zero))
    steps = lax.broadcasted_iota(jnp.int32, (BLOCK, channels), 0).astype(F32)
    for pole in range(POLES):
        rate = rates[pole : pole + 1]
        scale = weight[pole : pole + 1]
        ahead_ref[pole] = scale * jnp.exp(-(rate * steps))
        behind_ref[pole] = scale * jnp.exp(-(rate * (BLOCK - steps)))
    fade_ref[...] = jnp.exp(-(rates * BLOCK))


def group_kernel(length, width, near, index_ref, parts_ref, mixed, grad, log_ref, residue_ref, out_ref, *tables):
    rows = 3 * POLES

    @pl.when(index_ref[0] < EARLY)
    def _():
        local_part(length, mixed, grad, log_ref, residue_ref, *tables)

    fade = jnp.exp(-(own_rates(length, near, index_ref[0], log_ref) * width))
    places = [chunk ^ FLIP for chunk in range(near)]
    parts = [unpacked(parts_ref[at * rows : (at + 1) * rows, :].astype(F32)) for at in places]
    whole, _, _ = joined(parts, fade, width)
    end, start, end_moment, start_moment, res, rate = whole
    top = jnp.concatenate([end, start, end_moment], axis=0)
    low = jnp.concatenate([start_moment, res, rate], axis=0)
    sent = crossed(top, low)[0].astype(BF16)
    for at in range(out_ref.shape[0] // rows):
        out_ref[at * rows : (at + 1) * rows, :] = sent


def total_kernel(length, width, near, far_order, index_ref, parts_ref, groups_ref, log_ref, out_ref):
    rows = 3 * POLES
    index = index_ref[0]
    group = lax.div(index, near)
    rates = own_rates(length, near, index, log_ref)
    fade = jnp.exp(-(rates * width))
    groups = [None] * len(far_order)
    for at, member in enumerate(far_order):
        groups[member] = unpacked(groups_ref[at * rows : (at + 1) * rows, :].astype(F32))
    whole, ahead, behind = joined(groups, jnp.exp(-(rates * (width * near))), width * near)
    state, back = ahead[0], behind[0]
    for member in range(1, len(groups)):
        state = jnp.where(group == member, ahead[member], state)
        back = jnp.where(group == member, behind[member], back)
    states, backs = [], []
    for chunk in range(near):
        at = chunk ^ FLIP
        block = parts_ref[at * rows : (at + 1) * rows, :].astype(F32)
        states.append(state)
        state = fade * state + block[:POLES]
    for chunk in range(near - 1, -1, -1):
        at = chunk ^ FLIP
        block = parts_ref[at * rows : (at + 1) * rows, :].astype(F32)
        backs.append(back)
        back = fade * back + block[POLES : 2 * POLES]
    totals = jnp.concatenate(whole[4:], axis=0)
    rows = 2 * POLES
    for at in range(near):
        chunk = at ^ FLIP
        entering = jnp.concatenate([states[chunk], backs[near - 1 - chunk]], axis=0)
        out_ref[at * rows : (at + 1) * rows, :] = crossed(entering, totals)[0].astype(BF16)


def output_kernel(length, index_ref, carried_ref, *refs):
    early, (key_ref, value_ref, out_grad_ref, log_ref, residue_ref, mixed, grad), outs, late = (
        refs[:5],
        refs[5:12],
        refs[12:17],
        refs[17:],
    )
    residue_out, log_out = outs[3:]
    channels = residue_ref.shape[1]
    rates = jnp.exp(log_ref[...]) / length
    rate_scale = -(residue_ref[...] / length) * rates
    size = 2 * POLES
    states = []
    for half in range(channels // LANES):
        here = slice(half * LANES, (half + 1) * LANES)
        first, second = (carried_ref[at * size : (at + 1) * size, :].astype(F32) for at in (2 * half, 2 * half + 1))
        entering, totals = crossed(first, second)
        states.append(entering)
        residue_out[:, here] = totals[:POLES] * (1.0 / length)
        log_out[:, here] = rate_scale[:, here] * totals[POLES:]

    @pl.when(index_ref[0] < EARLY)
    def _():
        gate_gradients(states, early, key_ref, value_ref, out_grad_ref, *outs[:3])

    @pl.when(index_ref[0] >= EARLY)
    def _():
        local_part(length, mixed, grad, log_ref, residue_ref, *late)
        gate_gradients(states, late, key_ref, value_ref, out_grad_ref, *outs[:3])


def gate_gradients(states, tables, key_ref, value_ref, out_grad_ref, query_out, key_out, value_out):
    conv_ref, back_ref, ahead_ref, behind_ref, fade_ref = tables
    blocks = conv_ref.shape[0] // BLOCK
    for half, entering in enumerate(states):
        here = slice(half * LANES, (half + 1) * LANES)
        total = [conv_ref[block * BLOCK : (block + 1) * BLOCK, here] for block in range(blocks)]
        for pole in range(POLES):
            term = ahead_ref[pole, :, here] * entering[pole : pole + 1]
            fade = fade_ref[pole : pole + 1, here]
            for block in range(blocks):
                total[block] = total[block] + term
                term = term * fade
        conv = jnp.concatenate(total, axis=0).astype(BF16).T.astype(F32)
        query_out[here, :] = (out_grad_ref[here, :].astype(F32) * conv).astype(BF16)
        total = [back_ref[block * BLOCK : (block + 1) * BLOCK, here] for block in range(blocks)]
        for pole in range(POLES):
            term = behind_ref[pole, :, here] * entering[POLES + pole : POLES + pole + 1]
            fade = fade_ref[pole : pole + 1, here]
            for block in range(blocks - 1, -1, -1):
                total[block] = total[block] + term
                term = term * fade
        back = jnp.concatenate(total, axis=0).astype(BF16).T.astype(F32)
        key_out[here, :] = (back * value_ref[here, :].astype(F32)).astype(BF16)
        value_out[here, :] = (back * key_ref[here, :].astype(F32)).astype(BF16)


def on_device(query, key_gate, value_in, grad_output, residue, log_rate):
    chunks = lax.axis_size("ctx")
    channels, width = query.shape
    length = width * chunks
    struct = jax.ShapeDtypeStruct
    in_vmem = pl.BlockSpec(memory_space=pltpu.VMEM)
    in_smem = pl.BlockSpec(memory_space=pltpu.SMEM)
    in_hbm = pl.BlockSpec(memory_space=pltpu.HBM)
    params = pltpu.CompilerParams(vmem_limit_bytes=32 * MIB)
    gate, pole = struct((channels, width), BF16), struct((POLES, channels), F32)
    turned = struct((width, channels), F32)
    spread = struct((POLES, BLOCK, channels), F32)
    sources = [key_gate, value_in, query, grad_output, log_rate.T, residue.T]
    sources = [pltpu.with_memory_space_constraint(source, pltpu.HBM) for source in sources]
    tables = (turned, turned, spread, spread, pole)
    index = lax.axis_index("ctx").astype(jnp.int32).reshape(1)
    near, far = NEAR, chunks // NEAR
    rows = 3 * POLES
    far_order = [(5 * far // 8 - place) % far for place in range(far)]
    near_groups = [[group * near + (place ^ FLIP) for place in range(near)] for group in range(far)]
    far_groups = [[group * near + member for group in far_order] for member in range(near)]

    def exchange(table, groups):
        members = len(groups[0])
        shape = table.shape
        table = table.reshape(members, shape[0] // members, LANES)
        table = lax.all_to_all(table, "ctx", split_axis=0, concat_axis=0, axis_index_groups=groups, tiled=True)
        return table.reshape(shape)

    summary, key_gate, value_in, grad_output, logs, residues, mixed, grad = pl.pallas_call(
        functools.partial(summary_kernel, float(length)),
        out_shape=(struct((near * rows, LANES), BF16), gate, gate, gate, pole, pole, turned, turned),
        in_specs=[in_smem] + [in_hbm] * 6,
        out_specs=[in_vmem] * 8,
        scratch_shapes=[pltpu.VMEM(gate.shape, gate.dtype), pltpu.SemaphoreType.DMA((6, 2))],
        compiler_params=params,
        name="chunk_summary",
    )(index, *sources)
    parts = exchange(summary, near_groups)
    group, *early = pl.pallas_call(
        functools.partial(group_kernel, float(length), float(width), near),
        out_shape=(struct((far * rows, LANES), BF16), *tables),
        in_specs=[in_smem] + [in_vmem] * 5,
        out_specs=[in_vmem] * 6,
        compiler_params=params,
        name="group_summary",
    )(index, parts, mixed, grad, logs, residues)
    groups = exchange(group, far_groups)
    carried = pl.pallas_call(
        functools.partial(total_kernel, float(length), float(width), near, far_order),
        out_shape=struct((near * 2 * POLES, LANES), BF16),
        in_specs=[in_smem, in_vmem, in_vmem, in_vmem],
        out_specs=in_vmem,
        compiler_params=params,
        name="totals",
    )(index, parts, groups, logs)
    carried = exchange(carried, near_groups)
    outs = pl.pallas_call(
        functools.partial(output_kernel, float(length)),
        out_shape=(gate, gate, gate, pole, pole),
        in_specs=[in_smem] + [in_vmem] * 13,
        out_specs=[in_vmem] * 5,
        scratch_shapes=[pltpu.VMEM(table.shape, table.dtype) for table in tables],
        compiler_params=params,
        name="outputs",
    )(index, carried, *early, key_gate, value_in, grad_output, logs, residues, mixed, grad)
    return (*outs[:3], outs[3].T, outs[4].T)


def solution(mesh):
    both = P("ch", "ctx")
    rows = P("ch", None)
    return jax.shard_map(
        on_device,
        mesh=mesh,
        in_specs=(both, both, both, both, rows, rows),
        out_specs=(both, both, both, rows, rows),
        check_vma=False,
    )
```

```python
import functools

import jax
import jax.numpy as jnp
from jax import lax
from jax.experimental import pallas as pl
from jax.experimental.pallas import tpu as pltpu
from jax.sharding import PartitionSpec as P

F32 = jnp.float32
BF16 = jnp.bfloat16
POLES = 16
BLOCK = 8
LANES = 128
NEAR = 4
FLIP = 3
STEPS = 64
CHAINS = 4
EARLY = 8
MIB = 1024 * 1024


def gated(left_ref, right_ref):
    product = (left_ref[...].astype(F32) * right_ref[...].astype(F32)).astype(BF16)
    return product.T.astype(F32)


def crossed(first, second):
    left = lax.broadcasted_iota(jnp.int32, first.shape, 1) < LANES // 2
    return (
        jnp.where(left, first, pltpu.roll(second, LANES // 2, 1)),
        jnp.where(left, pltpu.roll(first, LANES // 2, 1), second),
    )


def unpacked(block):
    low = pltpu.roll(block, LANES // 2, 1)
    return [half[at * POLES : (at + 1) * POLES] for half in (block, low) for at in range(3)]


def joined(parts, fade, width):
    zero = jnp.zeros(fade.shape, F32)
    state, moment, res, rate = zero, zero, zero, zero
    ahead, behind = [], []
    for end, start, end_moment, start_moment, part_res, part_rate in parts:
        ahead.append(state)
        res = res + part_res + start * state
        rate = rate + part_rate + start_moment * state + start * moment
        moment = fade * (moment + width * state) + end_moment
        state = fade * state + end
    back, back_moment = zero, zero
    for _, start, _, start_moment, _, _ in parts[::-1]:
        behind.append(back)
        back_moment = fade * (back_moment + width * back) + start_moment
        back = fade * back + start
    return (state, back, moment, back_moment, res, rate), ahead, behind[::-1]


def own_rates(length, near, index, log_ref):
    block = jnp.bitwise_xor(lax.rem(index, near), FLIP)
    logs = jnp.where(block >= 2, log_ref[:, LANES:], log_ref[:, :LANES])
    logs = jnp.where(lax.rem(block, 2) == 1, pltpu.roll(logs, LANES // 2, 1), logs)
    return jnp.exp(logs) / length


def load_gates(sources, held, sems, mixed, grad):
    copies = [pltpu.make_async_copy(src, dst, sems.at[n]) for n, (src, dst) in enumerate(zip(sources, held))]
    for copy in copies:
        copy.start()
    copies[0].wait()
    copies[1].wait()
    mixed[...] = gated(held[0], held[1])
    copies[2].wait()
    copies[3].wait()
    grad[...] = gated(held[2], held[3])
    for copy in copies[4:]:
        copy.wait()


def summary_kernel(length, index_ref, *refs):
    sources, out_ref, held, (mixed, grad, query_ref, sems) = refs[:6], refs[6], refs[7:12], refs[12:]
    held = (*held[:2], query_ref, *held[2:])
    load_gates(sources, held, sems, mixed, grad)
    log_ref = held[4]
    width, channels = mixed.shape
    decay = jnp.exp(-(jnp.exp(log_ref[...]) / length))
    zero = jnp.zeros((POLES, channels), F32)

    def step(block, carry):
        state, moment, res, rate, back, back_moment = carry
        first = block * STEPS
        for row in range(STEPS):
            mixed_row = mixed[pl.ds(first + row, 1), :]
            grad_row = grad[pl.ds(first + row, 1), :]
            late_row = grad[pl.ds(width - 1 - first - row, 1), :]
            faded = decay * state
            state = faded + mixed_row
            moment = decay * moment + faded
            res = res + grad_row * state
            rate = rate + grad_row * moment
            faded = decay * back
            back = faded + late_row
            back_moment = decay * back_moment + faded
        return state, moment, res, rate, back, back_moment

    state, moment, res, rate, back, back_moment = lax.fori_loop(0, width // STEPS, step, (zero,) * 6)
    last = decay * state
    last_moment = decay * moment + last
    top = jnp.concatenate([last, back, last_moment], axis=0)
    low = jnp.concatenate([back_moment, res, rate], axis=0)
    rows = top.shape[0]
    for half in range(channels // LANES):
        here = slice(half * LANES, (half + 1) * LANES)
        pair = crossed(top[:, here], low[:, here])
        for side in range(2):
            block = 2 * half + side
            out_ref[block * rows : (block + 1) * rows, :] = pair[side].astype(BF16)


def local_part(length, mixed, grad, log_ref, residue_ref, conv_ref, back_ref, ahead_ref, behind_ref, fade_ref):
    width, channels = mixed.shape
    rates = jnp.exp(log_ref[...]) / length
    decay = jnp.exp(-rates)
    weight = residue_ref[...] * (length**-0.5)
    zero = jnp.zeros((POLES, channels), F32)

    def step(block, carry):
        state, back = carry
        first = pl.multiple_of(block * BLOCK, BLOCK)
        last = pl.multiple_of(width - BLOCK - block * BLOCK, BLOCK)
        ahead, behind = [], []
        for row in range(BLOCK):
            state = decay * state + mixed[pl.ds(first + row, 1), :]
            ahead.append(jnp.sum(weight * state, axis=0, keepdims=True))
            back = decay * back + grad[pl.ds(last + BLOCK - 1 - row, 1), :]
            behind.append(jnp.sum(weight * back, axis=0, keepdims=True))
        conv_ref[pl.ds(first, BLOCK), :] = jnp.concatenate(ahead, axis=0)
        back_ref[pl.ds(last, BLOCK), :] = jnp.concatenate(behind[::-1], axis=0)
        return state, back

    lax.fori_loop(0, width // BLOCK, step, (zero, zero))
    steps = lax.broadcasted_iota(jnp.int32, (BLOCK, channels), 0).astype(F32)
    for pole in range(POLES):
        rate = rates[pole : pole + 1]
        scale = weight[pole : pole + 1]
        ahead_ref[pole] = scale * jnp.exp(-(rate * steps))
        behind_ref[pole] = scale * jnp.exp(-(rate * (BLOCK - steps)))
    fade_ref[...] = jnp.exp(-(rates * BLOCK))


def group_kernel(length, width, near, index_ref, parts_ref, mixed, grad, log_ref, residue_ref, out_ref, *tables):
    rows = 3 * POLES

    @pl.when(index_ref[0] < EARLY)
    def _():
        local_part(length, mixed, grad, log_ref, residue_ref, *tables)

    fade = jnp.exp(-(own_rates(length, near, index_ref[0], log_ref) * width))
    places = [chunk ^ FLIP for chunk in range(near)]
    parts = [unpacked(parts_ref[at * rows : (at + 1) * rows, :].astype(F32)) for at in places]
    whole, _, _ = joined(parts, fade, width)
    end, start, end_moment, start_moment, res, rate = whole
    top = jnp.concatenate([end, start, end_moment], axis=0)
    low = jnp.concatenate([start_moment, res, rate], axis=0)
    sent = crossed(top, low)[0].astype(BF16)
    for at in range(out_ref.shape[0] // rows):
        out_ref[at * rows : (at + 1) * rows, :] = sent


def total_kernel(length, width, near, far_order, index_ref, parts_ref, groups_ref, log_ref, out_ref):
    rows = 3 * POLES
    index = index_ref[0]
    group = lax.div(index, near)
    rates = own_rates(length, near, index, log_ref)
    fade = jnp.exp(-(rates * width))
    groups = [None] * len(far_order)
    for at, member in enumerate(far_order):
        groups[member] = unpacked(groups_ref[at * rows : (at + 1) * rows, :].astype(F32))
    whole, ahead, behind = joined(groups, jnp.exp(-(rates * (width * near))), width * near)
    state, back = ahead[0], behind[0]
    for member in range(1, len(groups)):
        state = jnp.where(group == member, ahead[member], state)
        back = jnp.where(group == member, behind[member], back)
    states, backs = [], []
    for chunk in range(near):
        at = chunk ^ FLIP
        block = parts_ref[at * rows : (at + 1) * rows, :].astype(F32)
        states.append(state)
        state = fade * state + block[:POLES]
    for chunk in range(near - 1, -1, -1):
        at = chunk ^ FLIP
        block = parts_ref[at * rows : (at + 1) * rows, :].astype(F32)
        backs.append(back)
        back = fade * back + block[POLES : 2 * POLES]
    totals = jnp.concatenate(whole[4:], axis=0)
    rows = 2 * POLES
    for at in range(near):
        chunk = at ^ FLIP
        entering = jnp.concatenate([states[chunk], backs[near - 1 - chunk]], axis=0)
        out_ref[at * rows : (at + 1) * rows, :] = crossed(entering, totals)[0].astype(BF16)


def output_kernel(length, index_ref, carried_ref, *refs):
    early, (key_ref, value_ref, out_grad_ref, log_ref, residue_ref, mixed, grad), outs, late = (
        refs[:5],
        refs[5:12],
        refs[12:17],
        refs[17:],
    )
    residue_out, log_out = outs[3:]
    channels = residue_ref.shape[1]
    rates = jnp.exp(log_ref[...]) / length
    rate_scale = -(residue_ref[...] / length) * rates
    size = 2 * POLES
    states = []
    for half in range(channels // LANES):
        here = slice(half * LANES, (half + 1) * LANES)
        first, second = (carried_ref[at * size : (at + 1) * size, :].astype(F32) for at in (2 * half, 2 * half + 1))
        entering, totals = crossed(first, second)
        states.append(entering)
        residue_out[:, here] = totals[:POLES] * (1.0 / length)
        log_out[:, here] = rate_scale[:, here] * totals[POLES:]

    @pl.when(index_ref[0] < EARLY)
    def _():
        gate_gradients(states, early, key_ref, value_ref, out_grad_ref, *outs[:3])

    @pl.when(index_ref[0] >= EARLY)
    def _():
        local_part(length, mixed, grad, log_ref, residue_ref, *late)
        gate_gradients(states, late, key_ref, value_ref, out_grad_ref, *outs[:3])


def gate_gradients(states, tables, key_ref, value_ref, out_grad_ref, query_out, key_out, value_out):
    conv_ref, back_ref, ahead_ref, behind_ref, fade_ref = tables
    blocks = conv_ref.shape[0] // BLOCK
    for half, entering in enumerate(states):
        here = slice(half * LANES, (half + 1) * LANES)
        ahead = [conv_ref[block * BLOCK : (block + 1) * BLOCK, here] for block in range(blocks)]
        for pole in range(POLES):
            term = ahead_ref[pole, :, here] * entering[pole : pole + 1]
            spread(ahead, term, fade_ref[pole : pole + 1, here], range(blocks))
        conv = jnp.concatenate(ahead, axis=0).astype(BF16).T.astype(F32)
        query_out[here, :] = (out_grad_ref[here, :].astype(F32) * conv).astype(BF16)
        behind = [back_ref[block * BLOCK : (block + 1) * BLOCK, here] for block in range(blocks)]
        for pole in range(POLES):
            term = behind_ref[pole, :, here] * entering[POLES + pole : POLES + pole + 1]
            spread(behind, term, fade_ref[pole : pole + 1, here], range(blocks - 1, -1, -1))
        back = jnp.concatenate(behind, axis=0).astype(BF16).T.astype(F32)
        key_out[here, :] = (back * value_ref[here, :].astype(F32)).astype(BF16)
        value_out[here, :] = (back * key_ref[here, :].astype(F32)).astype(BF16)


def spread(total, term, fade, order):
    terms = [term]
    for _ in range(CHAINS - 1):
        terms.append(terms[-1] * fade)
    stride = fade
    for _ in range(CHAINS.bit_length() - 1):
        stride = stride * stride
    for place, block in enumerate(order):
        chain = place % CHAINS
        total[block] = total[block] + terms[chain]
        if place + CHAINS < len(order):
            terms[chain] = terms[chain] * stride


def on_device(query, key_gate, value_in, grad_output, residue, log_rate):
    chunks = lax.axis_size("ctx")
    channels, width = query.shape
    length = width * chunks
    struct = jax.ShapeDtypeStruct
    in_vmem = pl.BlockSpec(memory_space=pltpu.VMEM)
    in_smem = pl.BlockSpec(memory_space=pltpu.SMEM)
    in_hbm = pl.BlockSpec(memory_space=pltpu.HBM)
    params = pltpu.CompilerParams(vmem_limit_bytes=32 * MIB)
    gate, pole = struct((channels, width), BF16), struct((POLES, channels), F32)
    turned = struct((width, channels), F32)
    spread = struct((POLES, BLOCK, channels), F32)
    sources = [key_gate, value_in, query, grad_output, log_rate.T, residue.T]
    sources = [pltpu.with_memory_space_constraint(source, pltpu.HBM) for source in sources]
    tables = (turned, turned, spread, spread, pole)
    index = lax.axis_index("ctx").astype(jnp.int32).reshape(1)
    near, far = NEAR, chunks // NEAR
    rows = 3 * POLES
    far_order = [(5 * far // 8 - place) % far for place in range(far)]
    near_groups = [[group * near + (place ^ FLIP) for place in range(near)] for group in range(far)]
    far_groups = [[group * near + member for group in far_order] for member in range(near)]

    def exchange(table, groups):
        members = len(groups[0])
        shape = table.shape
        table = table.reshape(members, shape[0] // members, LANES)
        table = lax.all_to_all(table, "ctx", split_axis=0, concat_axis=0, axis_index_groups=groups, tiled=True)
        return table.reshape(shape)

    summary, key_gate, value_in, grad_output, logs, residues, mixed, grad = pl.pallas_call(
        functools.partial(summary_kernel, float(length)),
        out_shape=(struct((near * rows, LANES), BF16), gate, gate, gate, pole, pole, turned, turned),
        in_specs=[in_smem] + [in_hbm] * 6,
        out_specs=[in_vmem] * 8,
        scratch_shapes=[pltpu.VMEM(gate.shape, gate.dtype), pltpu.SemaphoreType.DMA((6,))],
        compiler_params=params,
        name="chunk_summary",
    )(index, *sources)
    parts = exchange(summary, near_groups)
    group, *early = pl.pallas_call(
        functools.partial(group_kernel, float(length), float(width), near),
        out_shape=(struct((far * rows, LANES), BF16), *tables),
        in_specs=[in_smem] + [in_vmem] * 5,
        out_specs=[in_vmem] * 6,
        compiler_params=params,
        name="group_summary",
    )(index, parts, mixed, grad, logs, residues)
    groups = exchange(group, far_groups)
    carried = pl.pallas_call(
        functools.partial(total_kernel, float(length), float(width), near, far_order),
        out_shape=struct((near * 2 * POLES, LANES), BF16),
        in_specs=[in_smem, in_vmem, in_vmem, in_vmem],
        out_specs=in_vmem,
        compiler_params=params,
        name="totals",
    )(index, parts, groups, logs)
    carried = exchange(carried, near_groups)
    outs = pl.pallas_call(
        functools.partial(output_kernel, float(length)),
        out_shape=(gate, gate, gate, pole, pole),
        in_specs=[in_smem] + [in_vmem] * 13,
        out_specs=[in_vmem] * 5,
        scratch_shapes=[pltpu.VMEM(table.shape, table.dtype) for table in tables],
        compiler_params=params,
        name="outputs",
    )(index, carried, *early, key_gate, value_in, grad_output, logs, residues, mixed, grad)
    return (*outs[:3], outs[3].T, outs[4].T)


def solution(mesh):
    both = P("ch", "ctx")
    rows = P("ch", None)
    return jax.shard_map(
        on_device,
        mesh=mesh,
        in_specs=(both, both, both, both, rows, rows),
        out_specs=(both, both, both, rows, rows),
        check_vma=False,
    )
```

```python
import functools

import jax
import jax.numpy as jnp
from jax import lax
from jax.experimental import pallas as pl
from jax.experimental.pallas import tpu as pltpu
from jax.sharding import PartitionSpec as P

F32 = jnp.float32
BF16 = jnp.bfloat16
POLES = 16
BLOCK = 8
LANES = 128
NEAR = 4
FLIP = 3
STEPS = 64
EARLY = 4
MIB = 1024 * 1024


def gated(left_ref, right_ref):
    product = (left_ref[...].astype(F32) * right_ref[...].astype(F32)).astype(BF16)
    return product.T.astype(F32)


def crossed(first, second):
    left = lax.broadcasted_iota(jnp.int32, first.shape, 1) < LANES // 2
    return (
        jnp.where(left, first, pltpu.roll(second, LANES // 2, 1)),
        jnp.where(left, pltpu.roll(first, LANES // 2, 1), second),
    )


def unpacked(block):
    low = pltpu.roll(block, LANES // 2, 1)
    return [half[at * POLES : (at + 1) * POLES] for half in (block, low) for at in range(3)]


def joined(parts, fade, width):
    zero = jnp.zeros(fade.shape, F32)
    state, moment, res, rate = zero, zero, zero, zero
    ahead, behind = [], []
    for end, start, end_moment, start_moment, part_res, part_rate in parts:
        ahead.append(state)
        res = res + part_res + start * state
        rate = rate + part_rate + start_moment * state + start * moment
        moment = fade * (moment + width * state) + end_moment
        state = fade * state + end
    back, back_moment = zero, zero
    for _, start, _, start_moment, _, _ in parts[::-1]:
        behind.append(back)
        back_moment = fade * (back_moment + width * back) + start_moment
        back = fade * back + start
    return (state, back, moment, back_moment, res, rate), ahead, behind[::-1]


def own_rates(length, near, index, log_ref):
    block = jnp.bitwise_xor(lax.rem(index, near), FLIP)
    logs = jnp.where(block >= 2, log_ref[:, LANES:], log_ref[:, :LANES])
    logs = jnp.where(lax.rem(block, 2) == 1, pltpu.roll(logs, LANES // 2, 1), logs)
    return jnp.exp(logs) / length


def load_gates(sources, held, sems, mixed, grad):
    copies = [pltpu.make_async_copy(src, dst, sems.at[n]) for n, (src, dst) in enumerate(zip(sources, held))]
    for copy in copies:
        copy.start()
    copies[0].wait()
    copies[1].wait()
    mixed[...] = gated(held[0], held[1])
    copies[2].wait()
    copies[3].wait()
    grad[...] = gated(held[2], held[3])
    for copy in copies[4:]:
        copy.wait()


def summary_kernel(length, index_ref, *refs):
    sources, out_ref, held, (mixed, grad, query_ref, sems) = refs[:6], refs[6], refs[7:12], refs[12:]
    held = (*held[:2], query_ref, *held[2:])
    load_gates(sources, held, sems, mixed, grad)
    log_ref = held[4]
    width, channels = mixed.shape
    decay = jnp.exp(-(jnp.exp(log_ref[...]) / length))
    zero = jnp.zeros((POLES, channels), F32)

    def step(block, carry):
        state, moment, res, rate, back, back_moment = carry
        first = block * STEPS
        for row in range(STEPS):
            mixed_row = mixed[pl.ds(first + row, 1), :]
            grad_row = grad[pl.ds(first + row, 1), :]
            late_row = grad[pl.ds(width - 1 - first - row, 1), :]
            faded = decay * state
            state = faded + mixed_row
            moment = decay * moment + faded
            res = res + grad_row * state
            rate = rate + grad_row * moment
            faded = decay * back
            back = faded + late_row
            back_moment = decay * back_moment + faded
        return state, moment, res, rate, back, back_moment

    state, moment, res, rate, back, back_moment = lax.fori_loop(0, width // STEPS, step, (zero,) * 6)
    last = decay * state
    last_moment = decay * moment + last
    top = jnp.concatenate([last, back, last_moment], axis=0)
    low = jnp.concatenate([back_moment, res, rate], axis=0)
    rows = top.shape[0]
    for half in range(channels // LANES):
        here = slice(half * LANES, (half + 1) * LANES)
        pair = crossed(top[:, here], low[:, here])
        for side in range(2):
            block = 2 * half + side
            out_ref[block * rows : (block + 1) * rows, :] = pair[side].astype(BF16)


def local_part(length, mixed, grad, log_ref, residue_ref, conv_ref, back_ref, ahead_ref, behind_ref, fade_ref):
    width, channels = mixed.shape
    rates = jnp.exp(log_ref[...]) / length
    decay = jnp.exp(-rates)
    weight = residue_ref[...] * (length**-0.5)
    zero = jnp.zeros((POLES, channels), F32)

    def step(block, carry):
        state, back = carry
        first = pl.multiple_of(block * BLOCK, BLOCK)
        last = pl.multiple_of(width - BLOCK - block * BLOCK, BLOCK)
        ahead, behind = [], []
        for row in range(BLOCK):
            state = decay * state + mixed[pl.ds(first + row, 1), :]
            ahead.append(jnp.sum(weight * state, axis=0, keepdims=True))
            back = decay * back + grad[pl.ds(last + BLOCK - 1 - row, 1), :]
            behind.append(jnp.sum(weight * back, axis=0, keepdims=True))
        conv_ref[pl.ds(first, BLOCK), :] = jnp.concatenate(ahead, axis=0)
        back_ref[pl.ds(last, BLOCK), :] = jnp.concatenate(behind[::-1], axis=0)
        return state, back

    lax.fori_loop(0, width // BLOCK, step, (zero, zero))
    steps = lax.broadcasted_iota(jnp.int32, (BLOCK, channels), 0).astype(F32)
    for pole in range(POLES):
        rate = rates[pole : pole + 1]
        scale = weight[pole : pole + 1]
        ahead_ref[pole] = scale * jnp.exp(-(rate * steps))
        behind_ref[pole] = scale * jnp.exp(-(rate * (BLOCK - steps)))
    fade_ref[...] = jnp.exp(-(rates * BLOCK))


def group_kernel(length, width, near, index_ref, parts_ref, mixed, grad, log_ref, residue_ref, out_ref, *tables):
    rows = 3 * POLES

    @pl.when(index_ref[0] < EARLY)
    def _():
        local_part(length, mixed, grad, log_ref, residue_ref, *tables)

    fade = jnp.exp(-(own_rates(length, near, index_ref[0], log_ref) * width))
    places = [chunk ^ FLIP for chunk in range(near)]
    parts = [unpacked(parts_ref[at * rows : (at + 1) * rows, :].astype(F32)) for at in places]
    whole, _, _ = joined(parts, fade, width)
    end, start, end_moment, start_moment, res, rate = whole
    top = jnp.concatenate([end, start, end_moment], axis=0)
    low = jnp.concatenate([start_moment, res, rate], axis=0)
    sent = crossed(top, low)[0].astype(BF16)
    for at in range(out_ref.shape[0] // rows):
        out_ref[at * rows : (at + 1) * rows, :] = sent


def total_kernel(length, width, near, far_order, index_ref, parts_ref, groups_ref, log_ref, out_ref):
    rows = 3 * POLES
    index = index_ref[0]
    group = lax.div(index, near)
    rates = own_rates(length, near, index, log_ref)
    fade = jnp.exp(-(rates * width))
    groups = [None] * len(far_order)
    for at, member in enumerate(far_order):
        groups[member] = unpacked(groups_ref[at * rows : (at + 1) * rows, :].astype(F32))
    whole, ahead, behind = joined(groups, jnp.exp(-(rates * (width * near))), width * near)
    state, back = ahead[0], behind[0]
    for member in range(1, len(groups)):
        state = jnp.where(group == member, ahead[member], state)
        back = jnp.where(group == member, behind[member], back)
    states, backs = [], []
    for chunk in range(near):
        at = chunk ^ FLIP
        block = parts_ref[at * rows : (at + 1) * rows, :].astype(F32)
        states.append(state)
        state = fade * state + block[:POLES]
    for chunk in range(near - 1, -1, -1):
        at = chunk ^ FLIP
        block = parts_ref[at * rows : (at + 1) * rows, :].astype(F32)
        backs.append(back)
        back = fade * back + block[POLES : 2 * POLES]
    totals = jnp.concatenate(whole[4:], axis=0)
    rows = 2 * POLES
    for at in range(near):
        chunk = at ^ FLIP
        entering = jnp.concatenate([states[chunk], backs[near - 1 - chunk]], axis=0)
        out_ref[at * rows : (at + 1) * rows, :] = crossed(entering, totals)[0].astype(BF16)


def output_kernel(length, index_ref, carried_ref, *refs):
    early, (key_ref, value_ref, out_grad_ref, log_ref, residue_ref, mixed, grad), outs, late = (
        refs[:5],
        refs[5:12],
        refs[12:17],
        refs[17:],
    )
    residue_out, log_out = outs[3:]
    channels = residue_ref.shape[1]
    rates = jnp.exp(log_ref[...]) / length
    rate_scale = -(residue_ref[...] / length) * rates
    size = 2 * POLES
    states = []
    for half in range(channels // LANES):
        here = slice(half * LANES, (half + 1) * LANES)
        first, second = (carried_ref[at * size : (at + 1) * size, :].astype(F32) for at in (2 * half, 2 * half + 1))
        entering, totals = crossed(first, second)
        states.append(entering)
        residue_out[:, here] = totals[:POLES] * (1.0 / length)
        log_out[:, here] = rate_scale[:, here] * totals[POLES:]

    @pl.when(index_ref[0] < EARLY)
    def _():
        gate_gradients(states, early, key_ref, value_ref, out_grad_ref, *outs[:3])

    @pl.when(index_ref[0] >= EARLY)
    def _():
        local_part(length, mixed, grad, log_ref, residue_ref, *late)
        gate_gradients(states, late, key_ref, value_ref, out_grad_ref, *outs[:3])


def gate_gradients(states, tables, key_ref, value_ref, out_grad_ref, query_out, key_out, value_out):
    conv_ref, back_ref, ahead_ref, behind_ref, fade_ref = tables
    blocks = conv_ref.shape[0] // BLOCK
    for half, entering in enumerate(states):
        here = slice(half * LANES, (half + 1) * LANES)
        total = [conv_ref[block * BLOCK : (block + 1) * BLOCK, here] for block in range(blocks)]
        for pole in range(POLES):
            term = ahead_ref[pole, :, here] * entering[pole : pole + 1]
            fade = fade_ref[pole : pole + 1, here]
            for block in range(blocks):
                total[block] = total[block] + term
                term = term * fade
        conv = jnp.concatenate(total, axis=0).astype(BF16).T.astype(F32)
        query_out[here, :] = (out_grad_ref[here, :].astype(F32) * conv).astype(BF16)
        total = [back_ref[block * BLOCK : (block + 1) * BLOCK, here] for block in range(blocks)]
        for pole in range(POLES):
            term = behind_ref[pole, :, here] * entering[POLES + pole : POLES + pole + 1]
            fade = fade_ref[pole : pole + 1, here]
            for block in range(blocks - 1, -1, -1):
                total[block] = total[block] + term
                term = term * fade
        back = jnp.concatenate(total, axis=0).astype(BF16).T.astype(F32)
        key_out[here, :] = (back * value_ref[here, :].astype(F32)).astype(BF16)
        value_out[here, :] = (back * key_ref[here, :].astype(F32)).astype(BF16)


def on_device(query, key_gate, value_in, grad_output, residue, log_rate):
    chunks = lax.axis_size("ctx")
    channels, width = query.shape
    length = width * chunks
    struct = jax.ShapeDtypeStruct
    in_vmem = pl.BlockSpec(memory_space=pltpu.VMEM)
    in_smem = pl.BlockSpec(memory_space=pltpu.SMEM)
    in_hbm = pl.BlockSpec(memory_space=pltpu.HBM)
    params = pltpu.CompilerParams(vmem_limit_bytes=32 * MIB)
    gate, pole = struct((channels, width), BF16), struct((POLES, channels), F32)
    turned = struct((width, channels), F32)
    spread = struct((POLES, BLOCK, channels), F32)
    sources = [key_gate, value_in, query, grad_output, log_rate.T, residue.T]
    sources = [pltpu.with_memory_space_constraint(source, pltpu.HBM) for source in sources]
    tables = (turned, turned, spread, spread, pole)
    index = lax.axis_index("ctx").astype(jnp.int32).reshape(1)
    near, far = NEAR, chunks // NEAR
    rows = 3 * POLES
    far_order = [(5 * far // 8 - place) % far for place in range(far)]
    near_groups = [[group * near + (place ^ FLIP) for place in range(near)] for group in range(far)]
    far_groups = [[group * near + member for group in far_order] for member in range(near)]

    def exchange(table, groups):
        members = len(groups[0])
        shape = table.shape
        table = table.reshape(members, shape[0] // members, LANES)
        table = lax.all_to_all(table, "ctx", split_axis=0, concat_axis=0, axis_index_groups=groups, tiled=True)
        return table.reshape(shape)

    summary, key_gate, value_in, grad_output, logs, residues, mixed, grad = pl.pallas_call(
        functools.partial(summary_kernel, float(length)),
        out_shape=(struct((near * rows, LANES), BF16), gate, gate, gate, pole, pole, turned, turned),
        in_specs=[in_smem] + [in_hbm] * 6,
        out_specs=[in_vmem] * 8,
        scratch_shapes=[pltpu.VMEM(gate.shape, gate.dtype), pltpu.SemaphoreType.DMA((6,))],
        compiler_params=params,
        name="chunk_summary",
    )(index, *sources)
    parts = exchange(summary, near_groups)
    group, *early = pl.pallas_call(
        functools.partial(group_kernel, float(length), float(width), near),
        out_shape=(struct((far * rows, LANES), BF16), *tables),
        in_specs=[in_smem] + [in_vmem] * 5,
        out_specs=[in_vmem] * 6,
        compiler_params=params,
        name="group_summary",
    )(index, parts, mixed, grad, logs, residues)
    groups = exchange(group, far_groups)
    carried = pl.pallas_call(
        functools.partial(total_kernel, float(length), float(width), near, far_order),
        out_shape=struct((near * 2 * POLES, LANES), BF16),
        in_specs=[in_smem, in_vmem, in_vmem, in_vmem],
        out_specs=in_vmem,
        compiler_params=params,
        name="totals",
    )(index, parts, groups, logs)
    carried = exchange(carried, near_groups)
    outs = pl.pallas_call(
        functools.partial(output_kernel, float(length)),
        out_shape=(gate, gate, gate, pole, pole),
        in_specs=[in_smem] + [in_vmem] * 13,
        out_specs=[in_vmem] * 5,
        scratch_shapes=[pltpu.VMEM(table.shape, table.dtype) for table in tables],
        compiler_params=params,
        name="outputs",
    )(index, carried, *early, key_gate, value_in, grad_output, logs, residues, mixed, grad)
    return (*outs[:3], outs[3].T, outs[4].T)


def solution(mesh):
    both = P("ch", "ctx")
    rows = P("ch", None)
    return jax.shard_map(
        on_device,
        mesh=mesh,
        in_specs=(both, both, both, both, rows, rows),
        out_specs=(both, both, both, rows, rows),
        check_vma=False,
    )
```
